256 devices in a mesh: cells: 32 (over y, z), modes: 8 (over x, core).
Axes of the slice: x: 4, y: 4, z: 8, core: 2. Of those that a mesh axis runs over, the one named last changes fastest.
Arguments:
- adjoint_source: float32 [128, 65536], P('modes', 'cells'), may hold values from -6 to 6
- coupling: float32 [9, 128, 128], replicated, may hold values from -0.5 to 0.5
- diag_blocks: bfloat16 [512, 9, 128, 128], P(('cells', 'modes')), may hold values from -0.125 to 0.125
- off_blocks: bfloat16 [512, 9, 128, 128], P(('cells', 'modes')), may hold values from -0.125 to 0.125
- owner_cells: int32 [512, 9, 1], P(('cells', 'modes')), may hold values from 0 to 31; in each aligned block of 18 rows (0 to 17, 18 to 35, ..., all dimensions but the last counted through in order) no two rows name the same one
- target_block: int32 [512, 9], P(('cells', 'modes')), may hold values from 0 to 15
Outputs:
- solution: float32 [128, 65536], P('modes', 'cells')
- next_basis: float32 [128, 65536], P('modes', 'cells')
The draws below stay inside these ranges and needn't reach their ends.
Inputs may be any that keep to these rules, and one draw needn't show every extreme that they name: `owner_cells`: among the 18 off-diagonal blocks of the rows of one device, at most 1 name the same owner, and in every draw some device's rows name some owner exactly 1 times.
All inputs are finite; a program needn't handle non-finite values.
Results may differ from the reference program's by a relative error of at most 0.004.
Values sent between devices are 32-bit elements; how exact they have to be, the bound alone decides.
A program may use at most 64 MiB of HBM per device.

```python
import math
import jax
import jax.numpy as jnp
import numpy as np
from jax import lax

P_SIZE = 128
TERMS = 9
BLOCK = 128
ITERS = 2
BPD = 2
SLAB = 16
NBLK = 512
CELLS = 65536
SLOTS = 1
N_CELLS = 32


def with_ends(result, own_key, low, largest):
    extent = result.shape
    place = [jax.random.randint(jax.random.fold_in(own_key, axis), (), 0, extent[axis]) for axis in range(len(extent))]
    result = result.at[tuple(place)].set(low)
    longest = extent.index(max(extent))
    place[longest] = (place[longest] + 1) % extent[longest]
    return result.at[tuple(place)].set(largest)


def block_scale(stream_key, shape, pieces, smallest, top_value):
    def one(axis_at, parts):
        draws = jax.random.uniform(jax.random.fold_in(jax.random.fold_in(stream_key, 6), axis_at), (parts,), jnp.float32, smallest / len(pieces), top_value / len(pieces))
        return jnp.repeat(jnp.exp(draws), shape[axis_at] // parts).reshape((-1,) + (1,) * (len(shape) - axis_at - 1))

    level = one(*pieces[0])
    for cut in pieces[1:]:
        level = level * one(*cut)
    return level


def assign_block(own_key, own, number, rows, amount, top, reach, lean):
    order = jax.random.permutation(own_key, amount)
    crowded, ordinary = portions_of(amount, rows * top, reach, lean, True), portions_of(amount, rows * top, reach, lean, False)
    places = jnp.arange(amount)

    def named(tallies, turn):
        used = int((tallies > 0).sum())
        fixed = max(1, used // 4)
        moved = fixed + (places - fixed + turn * (used - fixed)) % max(1, amount - fixed)
        return jnp.zeros((amount,), jnp.int32).at[order[jnp.where(places < fixed, places, moved)]].set(jnp.asarray(tallies, jnp.int32))

    tallies = jnp.where(number % 4 == 0, named(crowded, number // 4), named(ordinary, number - number // 4 - 1))
    mixed = jax.random.permutation(jax.random.fold_in(own, 3), amount)
    giver, taker = mixed[0:amount // 2 * 2:2], mixed[1:amount // 2 * 2:2]
    room = jnp.minimum(tallies[giver] - 1, reach - tallies[taker]) // 2
    room = jnp.where((giver == order[0]) | (taker == order[0]) | (tallies[taker] == 0), 0, jnp.maximum(room, 0))
    moved = jax.random.randint(jax.random.fold_in(own, 4), (amount // 2,), 0, 1 << 20) % (room + 1)
    tallies = tallies.at[giver].add(-moved).at[taker].add(moved)
    members = jnp.searchsorted(jnp.cumsum(tallies), jnp.arange(rows * top), side="right").astype(jnp.int32)
    grid = members.reshape(top, rows).T
    grid = grid[jax.random.permutation(jax.random.fold_in(own, 1), rows)]
    turn = jax.random.randint(jax.random.fold_in(own, 2), (rows, 1), 0, top)
    return jnp.take_along_axis(grid, (jnp.arange(top)[None, :] + turn) % top, axis=1)


def portions_of(count, total, limit, skew, full):
    portions = [(1 << 20) // math.isqrt(grade ** skew) + 1 for grade in range(1, count + 1)]
    largest = limit if full else min(limit, max(-(-total // count), total * portions[0] // sum(portions)))
    least = 1 if total - largest >= count - 1 else 0
    holding, rest = [largest] + [least] * (count - 1), total - largest - least * (count - 1)
    while rest > 0:
        candidates = [i for i in range(1, count) if holding[i] < largest] or [i for i in range(1, count) if holding[i] < limit]
        pool, left = sum([portions[i] for i in candidates]), rest
        for i in candidates:
            addition = min(limit - holding[i], max(1, left * portions[i] // pool), rest)
            holding[i] = holding[i] + addition
            rest = rest - addition
    return np.array(holding)


def scatter_about(rng, shape, scale, bound, shards=(), held_as=jnp.bfloat16):
    loudness = block_scale(rng, shape, shards, -0.22, 0.18) if shards else 1.0
    drawn = jax.random.normal(rng, shape, jnp.float32) * scale * loudness
    return jnp.minimum(jnp.maximum(drawn, -bound), bound).astype(held_as)


def setup_inputs(seed: int = 0) -> dict:
    splits = jax.random.split(jax.random.key(seed), 7)
    adjoint_source = scatter_about(splits[0], (P_SIZE, CELLS), 1.0, 6.0, ((0, 8), (1, 32)), jnp.float32)
    coupling = scatter_about(splits[1], (TERMS, P_SIZE, P_SIZE), P_SIZE ** -0.5, 0.5, (), jnp.float32)
    diag_blocks = scatter_about(splits[2], (NBLK, TERMS, BLOCK, BLOCK), (2 * TERMS * BLOCK) ** -0.5, 0.125, ((0, 256),))
    off_blocks = scatter_about(splits[3], (NBLK, TERMS, BLOCK, BLOCK), (2 * TERMS * BLOCK) ** -0.5, 0.125, ((0, 256),))
    owner_cells_keys = jax.random.split(jax.random.fold_in(splits[4], 1), NBLK * TERMS // (TERMS * BPD))
    owner_cells_turns = jax.random.permutation(jax.random.fold_in(splits[4], 3), NBLK * TERMS // (TERMS * BPD))
    owner_cells = jax.vmap(lambda own, number: assign_block(jax.random.fold_in(splits[4], 2), own, number, TERMS * BPD, N_CELLS, 1, SLOTS, 2))(owner_cells_keys, owner_cells_turns).reshape((NBLK, TERMS, 1))
    target_block = with_ends(jax.random.randint(splits[5], (NBLK, TERMS), 0, SLAB), jax.random.fold_in(splits[5], 1), 0, SLAB - 1).astype(jnp.int32)
    return {"adjoint_source": adjoint_source, "coupling": coupling, "diag_blocks": diag_blocks, "off_blocks": off_blocks, "owner_cells": owner_cells, "target_block": target_block}


def transposed_apply(vector_in, coupling, diag_blocks, off_blocks, owner_cells, target_block):
    block_total = diag_blocks.shape[0]
    targets = (owner_cells[:, :, 0] * SLAB + target_block).astype(jnp.int32)
    total = jnp.zeros((block_total, P_SIZE, BLOCK), jnp.float32)
    for term in range(TERMS):
        mixed_modes = jnp.dot(coupling[term].T, vector_in, precision=lax.Precision.HIGHEST, preferred_element_type=jnp.float32)
        rounded = lax.optimization_barrier(mixed_modes.astype(jnp.bfloat16))
        rounded = rounded.astype(jnp.float32).reshape(P_SIZE, block_total, BLOCK)
        near_terms = jnp.einsum('pbc,bcd->bpd', rounded, diag_blocks[:, term].astype(jnp.float32), precision=lax.Precision.HIGHEST)
        far_terms = jnp.einsum('pbc,bcd->bpd', rounded, off_blocks[:, term].astype(jnp.float32), precision=lax.Precision.HIGHEST)
        total = total + near_terms + jax.ops.segment_sum(far_terms, targets[:, term], num_segments=block_total)
    return total.transpose(1, 0, 2).reshape(P_SIZE, block_total * BLOCK)

def solve_small(columns, source_size):
    column_count = len(columns)
    rhs_terms = [source_size] + [source_size * 0.0 for unused in range(column_count)]
    cosines = []
    sine_list = []
    upper_cols = []
    for current in range(column_count):
        column = list(columns[current])
        for previous in range(current):
            first_val = column[previous]
            second_val = column[previous + 1]
            column[previous] = cosines[previous] * first_val + sine_list[previous] * second_val
            column[previous + 1] = cosines[previous] * second_val - sine_list[previous] * first_val
        radius = jnp.sqrt(column[current] * column[current] + column[current + 1] * column[current + 1])
        cosine = column[current] / radius
        sine_val = column[current + 1] / radius
        column[current] = radius
        rhs_terms[current + 1] = -sine_val * rhs_terms[current]
        rhs_terms[current] = cosine * rhs_terms[current]
        cosines.append(cosine)
        sine_list.append(sine_val)
        upper_cols.append(column)
    weights = [source_size] * column_count
    for current in reversed(range(column_count)):
        residue = rhs_terms[current]
        for later_idx in range(current + 1, column_count):
            residue = residue - upper_cols[later_idx][current] * weights[later_idx]
        weights[current] = residue / upper_cols[current][current]
    return weights

def reference(adjoint_source, coupling, diag_blocks, off_blocks, owner_cells, target_block):
    source_size = jnp.sqrt(jnp.sum(adjoint_source * adjoint_source))
    basis = [adjoint_source / source_size]
    columns = []
    for current in range(ITERS):
        candidate = transposed_apply(basis[current], coupling, diag_blocks, off_blocks, owner_cells, target_block)
        heights = []
        for vector in basis:
            product = jnp.sum(candidate * vector)
            candidate = candidate - product * vector
            heights.append(product)
        length = jnp.sqrt(jnp.sum(candidate * candidate))
        heights.append(length)
        columns.append(heights)
        basis.append(candidate / length)
    weights = solve_small(columns, source_size)
    solution = weights[0] * basis[0]
    for current in range(1, ITERS):
        solution = solution + weights[current] * basis[current]
    return (solution, source_size * basis[ITERS])
```

```python
import functools

import jax
import jax.numpy as jnp
from jax import lax
from jax.experimental import pallas as pl
from jax.experimental.pallas import tpu as pltpu
from jax.sharding import PartitionSpec as P

ITERS = 2
MESH = pl.DeviceIdType.MESH


def far_first(count):
    return sorted(range(count), key=lambda step: (-min(step, count - step), step))


def routing(owner_cells, target_block, cells_y, cells_z):
    entries = target_block.size
    owners = owner_cells.reshape(entries)
    targets = target_block.reshape(entries)
    here_z = lax.rem(lax.axis_index("cells"), cells_z)
    hop = lax.rem(lax.rem(owners, cells_z) - here_z + cells_z, cells_z)
    turn = sum(place * (hop == step).astype(jnp.int32) for place, step in enumerate(far_first(cells_z)))
    slot = turn * cells_y + owners // cells_z
    place = jnp.sum((slot[None, :] < slot[:, None]).astype(jnp.int32), axis=1)
    slots = cells_y * cells_z
    hit = slot[None, :] == jnp.arange(slots, dtype=jnp.int32)[:, None]
    there = jnp.any(hit, axis=1)
    where_from = jnp.where(there, jnp.sum(jnp.where(hit, place[None, :], 0), axis=1), entries)
    label = jnp.where(there, jnp.sum(jnp.where(hit, targets[None, :], 0), axis=1), -1)
    index = jnp.arange(entries, dtype=jnp.int32)
    order = jnp.sum(jnp.where(place[None, :] == index[:, None], index[None, :], 0), axis=1)
    table = jnp.concatenate([where_from, label, jnp.zeros((128 - 2 * slots,), jnp.int32)])
    return order, table.reshape(1, 128)


def kernel(
    dims,
    order_ref,
    table_ref,
    source_ref,
    coupling_ref,
    diag_ref,
    off_ref,
    solution_ref,
    next_ref,
    tables_row,
    tables_all,
    tables,
    regroup,
    raw,
    mixed,
    x_out,
    x_in_0,
    x_in_1,
    x_all,
    y_out,
    y_in,
    z_out,
    z_in,
    near_out,
    near_in,
    applied,
    sum_out,
    sum_x,
    sum_y,
    sum_z,
    table_sems,
    local_sem,
    regroup_sems,
    x_sems,
    y_sems,
    z_sems,
    near_sems,
    sum_x_sems,
    sum_y_sems,
    sum_z_sems,
):
    ny, nz, nm, terms, blocks_here = dims
    modes_total, block = coupling_ref.shape[1], off_ref.shape[-1]
    rows = modes_total // nm
    entries = terms * blocks_here
    slab = nm * blocks_here
    width = blocks_here * block
    turns = far_first(nz)
    cuts = [min(entries, ny * step) for step in range(nz + 1)]
    chunks = [(lo, hi) for lo, hi in zip(cuts[:-1], cuts[1:]) if hi > lo]
    x_in = (x_in_0, x_in_1)

    c = lax.axis_index("cells")
    m = lax.axis_index("modes")
    y, z = lax.div(c, nz), lax.rem(c, nz)

    def x_peer(d):
        return lax.rem(m + d, nm)

    def y_peer(d):
        return lax.rem(y + d, ny)

    def z_peer(d):
        return lax.rem(z + d, nz)

    def x_id(d):
        return (c, x_peer(d))

    def y_id(d):
        return (y_peer(d) * nz + z, m)

    def z_id(d):
        return (y * nz + z_peer(d), m)

    everyone = (
        [x_id(d) for d in range(1, nm)] + [y_id(d) for d in range(1, ny)] + [z_id(d) for d in range(1, nz)]
    )
    barrier = pltpu.get_barrier_semaphore()
    for device in everyone:
        pl.semaphore_signal(barrier, inc=1, device_id=device, device_id_type=MESH)

    started = []

    def send(src, dst, sems, device):
        copy = pltpu.make_async_remote_copy(
            src_ref=src,
            dst_ref=dst,
            send_sem=sems.at[0],
            recv_sem=sems.at[1],
            device_id=device,
            device_id_type=MESH,
        )
        copy.start()
        started.append(copy)

    def arrive(dst, sems, device):
        pltpu.make_async_remote_copy(
            src_ref=dst,
            dst_ref=dst,
            send_sem=sems.at[0],
            recv_sem=sems.at[1],
            device_id=device,
            device_id_type=MESH,
        ).wait_recv()

    def sum_start(at, tile):
        sum_out[at, 0] = tile
        sum_x[at, m] = tile
        for d in range(1, nm):
            send(sum_out.at[at, 0], sum_x.at[at, m], sum_x_sems.at[at, d], x_id(d))

    def sum_second(at):
        for d in range(1, nm):
            arrive(sum_x.at[at, x_peer(nm - d)], sum_x_sems.at[at, d], x_id(d))
        tile = sum_x[at, 0]
        for i in range(1, nm):
            tile = tile + sum_x[at, i]
        sum_out[at, 1] = tile
        sum_y[at, y] = tile
        for d in range(1, ny):
            send(sum_out.at[at, 1], sum_y.at[at, y], sum_y_sems.at[at, d], y_id(d))

    def sum_third(at):
        for d in range(1, ny):
            arrive(sum_y.at[at, y_peer(ny - d)], sum_y_sems.at[at, d], y_id(d))
        tile = sum_y[at, 0]
        for i in range(1, ny):
            tile = tile + sum_y[at, i]
        sum_out[at, 2] = tile
        sum_z[at, z] = tile
        for d in range(1, nz):
            send(sum_out.at[at, 2], sum_z.at[at, z], sum_z_sems.at[at, d], z_id(d))

    def sum_end(at):
        for d in range(1, nz):
            arrive(sum_z.at[at, z_peer(nz - d)], sum_z_sems.at[at, d], z_id(d))
        tile = sum_z[at, 0]
        for i in range(1, nz):
            tile = tile + sum_z[at, i]
        return jnp.sum(tile, axis=1, keepdims=True)

    def pack(lanes):
        line = lax.broadcasted_iota(jnp.int32, (8, 128), 0)
        tile = jnp.zeros((8, 128), jnp.float32)
        for i, value in enumerate(lanes):
            tile = jnp.where(line == i, jnp.broadcast_to(value, (8, 128)), tile)
        return tile

    def cell_block(ref, t):
        return ref[:, t * block : (t + 1) * block]

    def lanes_of(product):
        total = product(0)
        for t in range(1, slab):
            total = total + product(t)
        return jnp.sum(total, axis=0, keepdims=True)

    def regroup_start(at, src):
        for d in range(1, nm):
            columns = pl.ds(pl.multiple_of(x_peer(d) * width, width), width)
            send(src.at[:, columns], regroup.at[at, m], regroup_sems.at[at, d], x_id(d))
        own = pl.ds(pl.multiple_of(m * width, width), width)
        regroup[at, m] = src[:, own]

    def regroup_end(at):
        for d in range(1, nm):
            arrive(regroup.at[at, x_peer(nm - d)], regroup_sems.at[at, d], x_id(d))

    def mix(at, k):
        vector = regroup[at].reshape(modes_total, width)
        raw[at, k] = lax.dot_general(
            coupling_ref[k],
            vector,
            (((0,), (0,)), ((), ())),
            precision=lax.Precision.HIGHEST,
            preferred_element_type=jnp.float32,
        )

    def mix_and_sum(at):
        third = (terms + 2) // 3
        for k in range(0, third):
            mix(at, k)
        sum_second(at)
        for k in range(third, min(terms, 2 * third)):
            mix(at, k)
        sum_third(at)
        for k in range(min(terms, 2 * third), terms):
            mix(at, k)
        return sum_end(at)

    def far_and_near(at):
        landing = x_in[at]
        x_all[at, :, entries] = jnp.zeros((nm, rows, block), jnp.float32)
        for j, (lo, hi) in enumerate(chunks):
            for place in range(lo, hi):
                entry = order_ref[place]
                product = jnp.dot(mixed[entry], off_ref[entry], preferred_element_type=jnp.float32)
                x_out[at, place] = product.reshape(nm, rows, block)
            for d in range(1, nm):
                send(
                    x_out.at[at, lo:hi, x_peer(d)],
                    landing.at[m, lo:hi],
                    x_sems.at[at, j, d],
                    x_id(d),
                )
            x_all[at, m, lo:hi] = x_out[at, lo:hi, m]
        for b in range(blocks_here):
            total = jnp.dot(mixed[b * terms], diag_ref[b * terms], preferred_element_type=jnp.float32)
            for k in range(1, terms):
                total = total + jnp.dot(
                    mixed[b * terms + k], diag_ref[b * terms + k], preferred_element_type=jnp.float32
                )
            near_out[at, :, :, b * block : (b + 1) * block] = total.reshape(nm, rows, block)
        for d in range(1, nm):
            send(near_out.at[at, x_peer(d)], near_in.at[at, m], near_sems.at[at, d], x_id(d))
        near_in[at, m] = near_out[at, m]

        def hand_on(i):
            if i < len(chunks):
                lo, hi = chunks[i]
                for d in range(1, nm):
                    giver = x_peer(nm - d)
                    arrive(landing.at[giver, lo:hi], x_sems.at[at, i, d], x_id(d))
                    x_all[at, giver, lo:hi] = landing[giver, lo:hi]
            for d in range(ny):
                slot = i * ny + y_peer(d)
                for giver in range(nm):
                    tile = x_all[at, giver, tables[y, giver, 0, slot]]
                    if d:
                        y_out[at, i, d, giver] = tile
                    else:
                        y_in[at, i, y, giver] = tile
                if d:
                    send(y_out.at[at, i, d], y_in.at[at, i, y], y_sems.at[at, i, d], y_id(d))

        def gather(i):
            for d in range(1, ny):
                arrive(y_in.at[at, i, y_peer(ny - d)], y_sems.at[at, i, d], y_id(d))
            slot = ny * nz + i * ny + y

            def add(step, totals):
                giver_y, giver = lax.div(step, nm), lax.rem(step, nm)
                label = tables[giver_y, giver, 0, slot]
                tile = y_in[at, i, giver_y, giver]
                return tuple(total + jnp.where(label == t, tile, 0.0) for t, total in enumerate(totals))

            zero = jnp.zeros((rows, block), jnp.float32)
            totals = lax.fori_loop(0, ny * nm, add, (zero,) * slab)
            d = turns[i]
            for t in range(slab):
                if d:
                    z_out[at, i, t] = totals[t]
                else:
                    z_in[at, z, t] = totals[t]
            if d:
                send(z_out.at[at, i], z_in.at[at, z], z_sems.at[at, d], z_id(d))

        lag = 1
        for i in range(nz + lag):
            if i < nz:
                hand_on(i)
            if i >= lag:
                gather(i - lag)
        for d in range(1, nm):
            arrive(near_in.at[at, x_peer(nm - d)], near_sems.at[at, d], x_id(d))
        for d in range(1, nz):
            arrive(z_in.at[at, z_peer(nz - d)], z_sems.at[at, d], z_id(d))
        for t in range(slab):
            b = t % blocks_here
            total = near_in[at, t // blocks_here, :, b * block : (b + 1) * block]
            for giver in range(nz):
                total = total + z_in[at, giver, t]
            applied[at, :, t * block : (t + 1) * block] = total

    def round_mixed(value):
        for k in range(terms):
            rounded = value(k).astype(jnp.bfloat16)
            for b in range(blocks_here):
                mixed[b * terms + k] = rounded[:, b * block : (b + 1) * block]

    first, second = applied.at[0], applied.at[1]

    pl.semaphore_wait(barrier, len(everyone))
    regroup_start(0, source_ref)
    tables_row[m] = table_ref[...]
    for d in range(1, nm):
        send(table_ref, tables_row.at[m], table_sems.at[0, d], x_id(d))
    sum_start(0, pack([lanes_of(lambda t: cell_block(source_ref, t) * cell_block(source_ref, t))]))
    for d in range(1, nm):
        arrive(tables_row.at[x_peer(nm - d)], table_sems.at[0, d], x_id(d))
    tables_all[y] = tables_row[...]
    for d in range(1, ny):
        send(tables_row, tables_all.at[y], table_sems.at[1, d], y_id(d))
    regroup_end(0)
    sums = mix_and_sum(0)
    for d in range(1, ny):
        arrive(tables_all.at[y_peer(ny - d)], table_sems.at[1, d], y_id(d))
    tables_copy = pltpu.make_async_copy(tables_all, tables, local_sem)
    tables_copy.start()
    size = jnp.sqrt(sums[0:1])
    shrink = 1.0 / size
    round_mixed(lambda k: raw[0, k] * shrink)
    tables_copy.wait()
    far_and_near(0)

    regroup_start(1, first)
    sum_start(
        1,
        pack(
            [
                lanes_of(lambda t: cell_block(first, t) * cell_block(source_ref, t)),
                lanes_of(lambda t: cell_block(first, t) * cell_block(first, t)),
            ]
        ),
    )
    regroup_end(1)
    sums = mix_and_sum(1)
    h00 = sums[0:1] * shrink
    h10 = jnp.sqrt(jnp.maximum(sums[1:2] - h00 * h00, 0.0))
    lean = h00 * shrink
    shrink_1 = 1.0 / h10
    round_mixed(lambda k: (raw[1, k] - lean * raw[0, k]) * shrink_1)
    far_and_near(1)

    def basis_0(t):
        return cell_block(source_ref, t) * shrink

    def basis_1(t):
        return (cell_block(first, t) - lean * cell_block(source_ref, t)) * shrink_1

    sum_start(
        2,
        pack(
            [
                lanes_of(lambda t: cell_block(second, t) * basis_0(t)),
                lanes_of(lambda t: cell_block(second, t) * basis_1(t)),
                lanes_of(lambda t: cell_block(second, t) * cell_block(second, t)),
                lanes_of(lambda t: basis_0(t) * basis_1(t)),
                lanes_of(lambda t: basis_1(t) * basis_1(t)),
            ]
        ),
    )
    sum_second(2)
    sum_third(2)
    sums = sum_end(2)
    h01, cross = sums[0:1], sums[3:4]
    h11 = sums[1:2] - h01 * cross
    h21 = jnp.sqrt(
        jnp.maximum(
            sums[2:3]
            - 2.0 * h01 * h01
            - 2.0 * h11 * sums[1:2]
            + h01 * h01
            + h11 * h11 * sums[4:5]
            + 2.0 * h01 * h11 * cross,
            0.0,
        )
    )

    r00 = jnp.sqrt(h00 * h00 + h10 * h10)
    cos0, sin0 = h00 / r00, h10 / r00
    g1 = -sin0 * size
    g0 = cos0 * size
    r01 = cos0 * h01 + sin0 * h11
    low = cos0 * h11 - sin0 * h01
    r11 = jnp.sqrt(low * low + h21 * h21)
    g1 = (low / r11) * g1
    y1 = g1 / r11
    y0 = (g0 - r01 * y1) / r00
    grow = size / h21
    for t in range(slab):
        v0, v1 = basis_0(t), basis_1(t)
        solution_ref[:, t * block : (t + 1) * block] = y0 * v0 + y1 * v1
        next_ref[:, t * block : (t + 1) * block] = (cell_block(second, t) - h01 * v0 - h11 * v1) * grow

    for copy in started:
        copy.wait_send()


def body(cells_y, cells_z, adjoint_source, coupling, diag_blocks, off_blocks, owner_cells, target_block):
    nm = lax.axis_size("modes")
    blocks_here, terms, block = diag_blocks.shape[:3]
    modes_total = coupling.shape[1]
    entries = terms * blocks_here
    rows = modes_total // nm
    slab = nm * blocks_here
    width = blocks_here * block
    order, table = routing(owner_cells, target_block, cells_y, cells_z)
    dims = (cells_y, cells_z, nm, terms, blocks_here)
    f32 = jnp.float32
    chunk_count = -(-entries // cells_y)
    dma = pltpu.SemaphoreType.DMA
    vmem = pl.BlockSpec(memory_space=pltpu.VMEM)
    return pl.pallas_call(
        functools.partial(kernel, dims),
        out_shape=[jax.ShapeDtypeStruct(adjoint_source.shape, f32)] * 2,
        in_specs=[pl.BlockSpec(memory_space=pltpu.SMEM)] + [vmem] * 5,
        out_specs=[vmem, vmem],
        scratch_shapes=[
            pltpu.VMEM((nm, 1, 128), jnp.int32),
            pltpu.VMEM((cells_y, nm, 1, 128), jnp.int32),
            pltpu.SMEM((cells_y, nm, 1, 128), jnp.int32),
            pltpu.VMEM((2, nm, rows, width), f32),
            pltpu.VMEM((2, terms, modes_total, width), f32),
            pltpu.VMEM((entries, modes_total, block), jnp.bfloat16),
            pltpu.VMEM((2, entries, nm, rows, block), f32),
            pltpu.VMEM((nm, entries, rows, block), f32),
            pltpu.VMEM((nm, entries, rows, block), f32),
            pltpu.VMEM((2, nm, entries + 1, rows, block), f32),
            pltpu.VMEM((2, cells_z, cells_y, nm, rows, block), f32),
            pltpu.VMEM((2, cells_z, cells_y, nm, rows, block), f32),
            pltpu.VMEM((2, cells_z, slab, rows, block), f32),
            pltpu.VMEM((2, cells_z, slab, rows, block), f32),
            pltpu.VMEM((2, nm, rows, width), f32),
            pltpu.VMEM((2, nm, rows, width), f32),
            pltpu.VMEM((2, rows, slab * block), f32),
            pltpu.VMEM((3, 3, 8, 128), f32),
            pltpu.VMEM((3, nm, 8, 128), f32),
            pltpu.VMEM((3, cells_y, 8, 128), f32),
            pltpu.VMEM((3, cells_z, 8, 128), f32),
            dma((2, max(nm, cells_y), 2)),
            dma,
            dma((2, nm, 2)),
            dma((2, chunk_count, nm, 2)),
            dma((2, cells_z, cells_y, 2)),
            dma((2, cells_z, 2)),
            dma((2, nm, 2)),
            dma((3, nm, 2)),
            dma((3, cells_y, 2)),
            dma((3, cells_z, 2)),
        ],
        compiler_params=pltpu.CompilerParams(
            collective_id=0, has_side_effects=True, vmem_limit_bytes=48 * 1024 * 1024
        ),
    )(
        order,
        table,
        adjoint_source,
        coupling,
        diag_blocks.reshape(entries, block, block),
        off_blocks.reshape(entries, block, block),
    )


def solution(mesh, cells_z=8):
    cells_y = mesh.shape["cells"] // cells_z
    placed = (
        P("modes", "cells"),
        P(),
        P(("cells", "modes"), None, None, None),
        P(("cells", "modes"), None, None, None),
        P(("cells", "modes"), None, None),
        P(("cells", "modes"), None),
    )
    return jax.shard_map(
        functools.partial(body, cells_y, cells_z),
        mesh=mesh,
        in_specs=placed,
        out_specs=(P("modes", "cells"), P("modes", "cells")),
        check_vma=False,
    )
```

```python
import functools

import jax
import jax.numpy as jnp
from jax import lax
from jax.experimental import pallas as pl
from jax.experimental.pallas import tpu as pltpu
from jax.sharding import PartitionSpec as P

MESH = pl.DeviceIdType.MESH


def far_first(count):
    return sorted(range(count), key=lambda step: (-min(step, count - step), step))


def kernel(
    dims,
    owner_ref,
    target_ref,
    source_hbm,
    coupling_hbm,
    diag_hbm,
    off_hbm,
    solution_ref,
    next_ref,
    source_ref,
    coupling_ref,
    diag_ref,
    off_ref,
    load_sems,
    order_ref,
    table_out,
    tables_row,
    tables_all,
    sources,
    tables,
    regroup,
    mixers,
    mixed,
    x_out,
    x_in_0,
    x_in_1,
    x_all,
    y_out,
    y_in,
    z_out,
    z_in,
    near_out,
    near_in,
    far_sum,
    applied,
    sum_out,
    sum_x,
    sum_y,
    sum_z,
    table_sems,
    local_sems,
    regroup_sems,
    x_sems,
    y_sems,
    z_sems,
    near_sems,
    sum_x_sems,
    sum_y_sems,
    sum_z_sems,
):
    ny, nz, nm, terms, blocks_here = dims
    modes_total, block = coupling_ref.shape[1], off_ref.shape[-1]
    rows = modes_total // nm
    entries = terms * blocks_here
    slab = nm * blocks_here
    width = blocks_here * block
    turns = far_first(nz)
    turn_of = {d: i for i, d in enumerate(turns)}
    cuts = [min(entries, ny * step) for step in range(nz + 1)]
    chunks = [(lo, hi) for lo, hi in zip(cuts[:-1], cuts[1:]) if hi > lo]
    x_in = (x_in_0, x_in_1)

    c = lax.axis_index("cells")
    m = lax.axis_index("modes")
    y, z = lax.div(c, nz), lax.rem(c, nz)

    def x_peer(d):
        return lax.rem(m + d, nm)

    def y_peer(d):
        return lax.rem(y + d, ny)

    def z_peer(d):
        return lax.rem(z + d, nz)

    def x_id(d):
        return (c, x_peer(d))

    def y_id(d):
        return (y_peer(d) * nz + z, m)

    def z_id(d):
        return (y * nz + z_peer(d), m)

    everyone = (
        [x_id(d) for d in range(1, nm)]
        + [y_id(d) for d in range(1, ny)]
        + [z_id(d) for d in sorted({1, nz - 1})]
    )
    barrier = pltpu.get_barrier_semaphore()
    for device in everyone:
        pl.semaphore_signal(barrier, inc=1, device_id=device, device_id_type=MESH)
    loads = [
        pltpu.make_async_copy(src, dst, load_sems.at[i])
        for i, (src, dst) in enumerate(
            [
                (source_hbm, source_ref),
                (coupling_hbm, coupling_ref),
                (off_hbm, off_ref),
                (diag_hbm, diag_ref),
            ]
        )
    ]
    for load in loads:
        load.start()

    started = []

    def send(src, dst, sems, device):
        copy = pltpu.make_async_remote_copy(
            src_ref=src,
            dst_ref=dst,
            send_sem=sems.at[0],
            recv_sem=sems.at[1],
            device_id=device,
            device_id_type=MESH,
        )
        copy.start()
        started.append(copy)

    def arrive(dst, sems, device):
        pltpu.make_async_remote_copy(
            src_ref=dst,
            dst_ref=dst,
            send_sem=sems.at[0],
            recv_sem=sems.at[1],
            device_id=device,
            device_id_type=MESH,
        ).wait_recv()

    def sum_all(tile):
        stages = (
            (sum_x, sum_x_sems, m, nm, x_peer, x_id),
            (sum_y, sum_y_sems, y, ny, y_peer, y_id),
            (sum_z, sum_z_sems, z, nz, z_peer, z_id),
        )
        for at, (held, sems, here, count, peer, device) in enumerate(stages):
            sum_out[at] = tile
            for d in range(1, count):
                send(sum_out.at[at], held.at[here], sems.at[d], device(d))
            held[here] = tile
            for d in range(1, count):
                arrive(held.at[peer(count - d)], sems.at[d], device(d))
            tile = held[0]
            for i in range(1, count):
                tile = tile + held[i]
        return jnp.sum(tile, axis=1, keepdims=True)

    def pack(lanes):
        line = lax.broadcasted_iota(jnp.int32, (8, 128), 0)
        tile = jnp.zeros((8, 128), jnp.float32)
        for i, value in enumerate(lanes):
            tile = jnp.where(line == i, jnp.broadcast_to(value, (8, 128)), tile)
        return tile

    def cell_block(ref, t):
        return ref[:, t * block : (t + 1) * block]

    def dot_lanes(left, right):
        total = cell_block(left, 0) * cell_block(right, 0)
        for t in range(1, slab):
            total = total + cell_block(left, t) * cell_block(right, t)
        return jnp.sum(total, axis=0, keepdims=True)

    def regroup_start(at, src):
        for d in range(1, nm):
            columns = pl.ds(pl.multiple_of(x_peer(d) * width, width), width)
            send(src.at[:, columns], regroup.at[at, m], regroup_sems.at[at, d], x_id(d))
        own = pl.ds(pl.multiple_of(m * width, width), width)
        regroup[at, m] = src[:, own]

    def regroup_end(at):
        for d in range(1, nm):
            arrive(regroup.at[at, x_peer(nm - d)], regroup_sems.at[at, d], x_id(d))
        return regroup[at].reshape(modes_total, width)

    def split(value):
        high = value.astype(jnp.bfloat16)
        return high, (value - high.astype(jnp.float32)).astype(jnp.bfloat16)

    def mix(vector):
        high, low = split(vector)
        stacked = jnp.concatenate([high, high, low], axis=0)
        for k in range(terms):
            value = jnp.dot(mixers[k], stacked, preferred_element_type=jnp.float32)
            high_k, low_k = split(value)
            for b in range(blocks_here):
                mixed[b * terms + k, 0] = high_k[:, b * block : (b + 1) * block]
                mixed[b * terms + k, 1] = low_k[:, b * block : (b + 1) * block]

    def times(entry, blocks, at_block):
        matrix = blocks[at_block]
        return jnp.dot(mixed[entry, 0], matrix, preferred_element_type=jnp.float32) + jnp.dot(
            mixed[entry, 1], matrix, preferred_element_type=jnp.float32
        )

    def far_and_near(at, know_row=lambda: None, know_all=lambda: None):
        landing = x_in[at]
        x_all[at, :, entries] = jnp.zeros((nm, rows, block), jnp.float32)
        for j, (lo, hi) in enumerate(chunks):
            for place in range(lo, hi):
                entry = order_ref[place]
                x_out[at, place] = times(entry, off_ref, entry).reshape(nm, rows, block)
            for d in range(1, nm):
                send(
                    x_out.at[at, lo:hi, x_peer(d)],
                    landing.at[m, lo:hi],
                    x_sems.at[at, j, d],
                    x_id(d),
                )
            x_all[at, m, lo:hi] = x_out[at, lo:hi, m]

        def near():
            for b in range(blocks_here):
                total = times(b * terms, diag_ref, b * terms)
                for k in range(1, terms):
                    total = total + times(b * terms + k, diag_ref, b * terms + k)
                near_out[at, :, :, b * block : (b + 1) * block] = total.reshape(nm, rows, block)
            for d in range(1, nm):
                send(near_out.at[at, x_peer(d)], near_in.at[at, m], near_sems.at[at, d], x_id(d))
            near_in[at, m] = near_out[at, m]

        def hand_on(i):
            if i < len(chunks):
                lo, hi = chunks[i]
                for d in range(1, nm):
                    giver = x_peer(nm - d)
                    arrive(landing.at[giver, lo:hi], x_sems.at[at, i, d], x_id(d))
                    x_all[at, giver, lo:hi] = landing[giver, lo:hi]
            for d in list(range(1, ny)) + [0]:
                slot = i * ny + y_peer(d)
                for giver in range(nm):
                    tile = x_all[at, giver, sources[giver, 0, slot]]
                    if d:
                        y_out[at, i, d, giver] = tile
                    else:
                        y_in[at, i, y, giver] = tile
                if d:
                    send(y_out.at[at, i, d], y_in.at[at, i, y], y_sems.at[at, i, d], y_id(d))

        half = slab // 2
        up, down = (0, slice(0, half)), (1, slice(half, slab))

        def z_received(way, d, targets):
            came_from = d + 1 if way == 0 else (d - 1) % nz
            step = nz - 1 if way == 0 else 1
            held = z_in.at[at, way, turn_of[came_from], targets]
            arrive(held, z_sems.at[at, way, turn_of[came_from]], z_id(step))
            return held

        def gather(i):
            for d in range(1, ny):
                arrive(y_in.at[at, i, y_peer(ny - d)], y_sems.at[at, i, d], y_id(d))
            slot = ny * nz + i * ny + y

            def add(step, totals):
                giver_y, giver = lax.div(step, nm), lax.rem(step, nm)
                label = tables[giver_y, giver, 0, slot]
                tile = y_in[at, i, giver_y, giver]
                return tuple(total + jnp.where(label == t, tile, 0.0) for t, total in enumerate(totals))

            zero = jnp.zeros((rows, block), jnp.float32)
            totals = list(lax.fori_loop(0, ny * nm, add, (zero,) * slab))
            d = turns[i]
            middle = nz // 2
            everything = slice(0, slab)
            if d < middle:
                targets = up[1] if d + 1 == middle else everything
                held = z_received(0, d, targets)
                for t in range(targets.start, targets.stop):
                    totals[t] = totals[t] + held[t - targets.start]
            if d > middle or d == 0:
                targets = down[1] if (d - 1) % nz == middle else everything
                held = z_received(1, d, targets)
                for t in range(targets.start, targets.stop):
                    totals[t] = totals[t] + held[t - targets.start]
            if d == 0:
                for t in range(slab):
                    far_sum[at, :, t * block : (t + 1) * block] = totals[t]
                return
            for t in range(slab):
                z_out[at, i, t] = totals[t]
            if d <= middle:
                targets = up[1] if d == middle else everything
                send(z_out.at[at, i, targets], z_in.at[at, 0, i, targets], z_sems.at[at, 0, i], z_id(1))
            if d >= middle:
                targets = down[1] if d == middle else everything
                send(z_out.at[at, i, targets], z_in.at[at, 1, i, targets], z_sems.at[at, 1, i], z_id(nz - 1))

        know_row()
        lag = min(2, nz)
        for i in range(nz + lag):
            if i < nz:
                hand_on(i)
            if i == 1:
                near()
                know_all()
            if i >= lag:
                gather(i - lag)

    def complete(at):
        for d in range(1, nm):
            arrive(near_in.at[at, x_peer(nm - d)], near_sems.at[at, d], x_id(d))
        for t in range(slab):
            b = t % blocks_here
            applied[at, :, t * block : (t + 1) * block] = (
                near_in[at, t // blocks_here, :, b * block : (b + 1) * block] + far_sum[at, :, t * block : (t + 1) * block]
            )

    slots = ny * nz
    slot_of, target_of = [], []
    for e in range(entries):
        owner = owner_ref[e // terms, 0, e % terms]
        hop = lax.rem(lax.rem(owner, nz) - z + nz, nz)
        near_hop = jnp.minimum(hop, nz - hop)
        turn = jnp.maximum(nz - 2 * near_hop - jnp.where(2 * hop <= nz, 1, 0), 0)
        slot_of.append(turn * ny + lax.div(owner, nz))
        target_of.append(target_ref[e // terms, e % terms])
    place_of = []
    for e in range(entries):
        place = jnp.int32(0)
        for other in range(entries):
            if other != e:
                place = place + jnp.where(slot_of[other] < slot_of[e], 1, 0)
        place_of.append(place)
    for p in range(entries):
        entry = jnp.int32(0)
        for e in range(1, entries):
            entry = entry + jnp.where(place_of[e] == p, e, 0)
        order_ref[p] = jnp.minimum(entry, entries - 1)
    lane = lax.broadcasted_iota(jnp.int32, (1, 128), 1)
    there = jnp.zeros((1, 128), jnp.int32)
    before = jnp.zeros((1, 128), jnp.int32)
    label = jnp.full((1, 128), -1, jnp.int32)
    for e in range(entries):
        there = there + jnp.where(lane == slot_of[e], 1, 0)
        before = before + jnp.where(lane > slot_of[e], 1, 0)
        label = jnp.where(lane - slots == slot_of[e], target_of[e], label)
    table_out[...] = jnp.where(lane < slots, jnp.where(there > 0, before, entries), label)

    loads[0].wait()
    pl.semaphore_wait(barrier, len(everyone))
    regroup_start(0, source_ref)
    for d in range(1, nm):
        send(table_out, tables_row.at[m], table_sems.at[0, d], x_id(d))
    tables_row[m] = table_out[...]
    loads[1].wait()
    for k in range(terms):
        high, low = split(coupling_ref[k].T)
        mixers[k] = jnp.concatenate([high, low, high], axis=1)
    for d in range(1, nm):
        arrive(tables_row.at[x_peer(nm - d)], table_sems.at[0, d], x_id(d))
    for d in range(1, ny):
        send(tables_row, tables_all.at[y], table_sems.at[1, d], y_id(d))
    row_copy = pltpu.make_async_copy(tables_row, sources, local_sems.at[0])
    row_copy.start()
    tables_all[y] = tables_row[...]
    mix(regroup_end(0))
    loads[2].wait()
    loads[3].wait()

    def know_row():
        row_copy.wait()

    def know_all():
        for d in range(1, ny):
            arrive(tables_all.at[y_peer(ny - d)], table_sems.at[1, d], y_id(d))
        all_copy = pltpu.make_async_copy(tables_all, tables, local_sems.at[1])
        all_copy.start()
        all_copy.wait()

    far_and_near(0, know_row, know_all)

    regroup_start(1, far_sum.at[0])
    far = regroup_end(1)
    mix(far + near_out[0].reshape(modes_total, width))
    far_and_near(1)
    complete(0)
    complete(1)
    first, second = applied.at[0], applied.at[1]

    sums = sum_all(
        pack(
            [
                dot_lanes(source_ref, source_ref),
                dot_lanes(source_ref, first),
                dot_lanes(first, first),
                dot_lanes(source_ref, second),
                dot_lanes(first, second),
                dot_lanes(second, second),
            ]
        )
    )
    uu, uw, ww, uq, wq, qq = (sums[i : i + 1] for i in range(6))
    size = jnp.sqrt(uu)
    h00 = uw / uu
    h10 = jnp.sqrt(jnp.maximum(ww / uu - h00 * h00, 0.0))
    scale = 1.0 / h10
    h01 = (uq - h00 * uw) / uu * scale
    h11 = (wq - h00 * uq - h00 * (ww - h00 * uw)) / uu * scale * scale
    h21 = jnp.sqrt(
        jnp.maximum(
            (qq - 2.0 * h00 * wq + h00 * h00 * ww) / uu * scale * scale - h01 * h01 - h11 * h11,
            0.0,
        )
    )

    r00 = jnp.sqrt(h00 * h00 + h10 * h10)
    cos0, sin0 = h00 / r00, h10 / r00
    g1 = -sin0 * size
    g0 = cos0 * size
    r01 = cos0 * h01 + sin0 * h11
    low = cos0 * h11 - sin0 * h01
    r11 = jnp.sqrt(low * low + h21 * h21)
    y1 = (low / r11) * g1 / r11
    y0 = (g0 - r01 * y1) / r00

    sol_w = y1 * scale / size
    sol_u = y0 / size - sol_w * h00
    next_q = scale / h21
    next_w = -(h00 + h11) * next_q
    next_u = h11 * h00 * next_q - h01 / h21
    for t in range(slab):
        u, w = cell_block(source_ref, t), cell_block(first, t)
        solution_ref[:, t * block : (t + 1) * block] = sol_u * u + sol_w * w
        next_ref[:, t * block : (t + 1) * block] = next_q * cell_block(second, t) + next_w * w + next_u * u

    for copy in started:
        copy.wait_send()


def body(cells_y, cells_z, adjoint_source, coupling, diag_blocks, off_blocks, owner_cells, target_block):
    nm = lax.axis_size("modes")
    blocks_here, terms, block = diag_blocks.shape[:3]
    modes_total = coupling.shape[1]
    entries = terms * blocks_here
    rows = modes_total // nm
    slab = nm * blocks_here
    width = blocks_here * block
    dims = (cells_y, cells_z, nm, terms, blocks_here)
    f32, bf16 = jnp.float32, jnp.bfloat16
    chunk_count = -(-entries // cells_y)
    dma = pltpu.SemaphoreType.DMA
    vmem = pl.BlockSpec(memory_space=pltpu.VMEM)
    smem = pl.BlockSpec(memory_space=pltpu.SMEM)
    anywhere = pl.BlockSpec(memory_space=pl.ANY)
    return pl.pallas_call(
        functools.partial(kernel, dims),
        out_shape=[jax.ShapeDtypeStruct(adjoint_source.shape, f32)] * 2,
        in_specs=[smem, smem] + [anywhere] * 4,
        out_specs=[vmem, vmem],
        scratch_shapes=[
            pltpu.VMEM((rows, slab * block), f32),
            pltpu.VMEM((terms, modes_total, modes_total), f32),
            pltpu.VMEM((entries, block, block), bf16),
            pltpu.VMEM((entries, block, block), bf16),
            dma((4,)),
            pltpu.SMEM((entries,), jnp.int32),
            pltpu.VMEM((1, 128), jnp.int32),
            pltpu.VMEM((nm, 1, 128), jnp.int32),
            pltpu.VMEM((cells_y, nm, 1, 128), jnp.int32),
            pltpu.SMEM((nm, 1, 128), jnp.int32),
            pltpu.SMEM((cells_y, nm, 1, 128), jnp.int32),
            pltpu.VMEM((2, nm, rows, width), f32),
            pltpu.VMEM((terms, modes_total, 3 * modes_total), bf16),
            pltpu.VMEM((entries, 2, modes_total, block), bf16),
            pltpu.VMEM((2, entries, nm, rows, block), f32),
            pltpu.VMEM((nm, entries, rows, block), f32),
            pltpu.VMEM((nm, entries, rows, block), f32),
            pltpu.VMEM((2, nm, entries + 1, rows, block), f32),
            pltpu.VMEM((2, cells_z, cells_y, nm, rows, block), f32),
            pltpu.VMEM((2, cells_z, cells_y, nm, rows, block), f32),
            pltpu.VMEM((2, cells_z, slab, rows, block), f32),
            pltpu.VMEM((2, 2, cells_z, slab, rows, block), f32),
            pltpu.VMEM((2, nm, rows, width), f32),
            pltpu.VMEM((2, nm, rows, width), f32),
            pltpu.VMEM((2, rows, slab * block), f32),
            pltpu.VMEM((2, rows, slab * block), f32),
            pltpu.VMEM((3, 8, 128), f32),
            pltpu.VMEM((nm, 8, 128), f32),
            pltpu.VMEM((cells_y, 8, 128), f32),
            pltpu.VMEM((cells_z, 8, 128), f32),
            dma((2, max(nm, cells_y), 2)),
            dma((2,)),
            dma((2, nm, 2)),
            dma((2, chunk_count, nm, 2)),
            dma((2, cells_z, cells_y, 2)),
            dma((2, 2, cells_z, 2)),
            dma((2, nm, 2)),
            dma((nm, 2)),
            dma((cells_y, 2)),
            dma((cells_z, 2)),
        ],
        compiler_params=pltpu.CompilerParams(
            collective_id=0, has_side_effects=True, vmem_limit_bytes=62 * 1024 * 1024
        ),
    )(
        owner_cells.transpose(0, 2, 1),
        target_block,
        adjoint_source,
        coupling,
        diag_blocks.reshape(entries, block, block),
        off_blocks.reshape(entries, block, block),
    )


def solution(mesh, cells_z=8):
    cells_y = mesh.shape["cells"] // cells_z
    placed = (
        P("modes", "cells"),
        P(),
        P(("cells", "modes"), None, None, None),
        P(("cells", "modes"), None, None, None),
        P(("cells", "modes"), None, None),
        P(("cells", "modes"), None),
    )
    return jax.shard_map(
        functools.partial(body, cells_y, cells_z),
        mesh=mesh,
        in_specs=placed,
        out_specs=(P("modes", "cells"), P("modes", "cells")),
        check_vma=False,
    )
```

```python
import functools

import jax
import jax.numpy as jnp
from jax import lax
from jax.experimental import pallas as pl
from jax.experimental.pallas import tpu as pltpu
from jax.sharding import PartitionSpec as P

MESH = pl.DeviceIdType.MESH


def far_first(count):
    return sorted(range(count), key=lambda step: (-min(step, count - step), step))


def kernel(
    dims,
    owner_ref,
    target_ref,
    source_hbm,
    coupling_hbm,
    diag_hbm,
    off_hbm,
    solution_ref,
    next_ref,
    source_ref,
    coupling_ref,
    diag_ref,
    off_ref,
    load_sems,
    order_ref,
    table_out,
    tables_row,
    tables_all,
    sources,
    tables,
    regroup,
    raw,
    mixed,
    x_out,
    x_in_0,
    x_in_1,
    x_all,
    y_out,
    y_in,
    z_out,
    z_in,
    near_out,
    near_in,
    far_sum,
    applied,
    sum_out,
    sum_x,
    sum_y,
    sum_z,
    table_sems,
    local_sems,
    regroup_sems,
    x_sems,
    y_sems,
    z_sems,
    near_sems,
    sum_x_sems,
    sum_y_sems,
    sum_z_sems,
):
    ny, nz, nm, terms, blocks_here = dims
    modes_total, block = coupling_ref.shape[1], off_ref.shape[-1]
    rows = modes_total // nm
    entries = terms * blocks_here
    slab = nm * blocks_here
    width = blocks_here * block
    turns = far_first(nz)
    turn_of = {d: i for i, d in enumerate(turns)}
    cuts = [min(entries, ny * step) for step in range(nz + 1)]
    chunks = [(lo, hi) for lo, hi in zip(cuts[:-1], cuts[1:]) if hi > lo]
    x_in = (x_in_0, x_in_1)

    c = lax.axis_index("cells")
    m = lax.axis_index("modes")
    y, z = lax.div(c, nz), lax.rem(c, nz)

    def x_peer(d):
        return lax.rem(m + d, nm)

    def y_peer(d):
        return lax.rem(y + d, ny)

    def z_peer(d):
        return lax.rem(z + d, nz)

    def x_id(d):
        return (c, x_peer(d))

    def y_id(d):
        return (y_peer(d) * nz + z, m)

    def z_id(d):
        return (y * nz + z_peer(d), m)

    everyone = (
        [x_id(d) for d in range(1, nm)]
        + [y_id(d) for d in range(1, ny)]
        + [z_id(d) for d in range(1, nz)]
    )
    barrier = pltpu.get_barrier_semaphore()
    for device in everyone:
        pl.semaphore_signal(barrier, inc=1, device_id=device, device_id_type=MESH)
    loads = [
        pltpu.make_async_copy(src, dst, load_sems.at[i])
        for i, (src, dst) in enumerate(
            [
                (source_hbm, source_ref),
                (coupling_hbm, coupling_ref),
                (off_hbm, off_ref),
                (diag_hbm, diag_ref),
            ]
        )
    ]
    for load in loads:
        load.start()

    started = []

    def send(src, dst, sems, device):
        copy = pltpu.make_async_remote_copy(
            src_ref=src,
            dst_ref=dst,
            send_sem=sems.at[0],
            recv_sem=sems.at[1],
            device_id=device,
            device_id_type=MESH,
        )
        copy.start()
        started.append(copy)

    def arrive(dst, sems, device):
        pltpu.make_async_remote_copy(
            src_ref=dst,
            dst_ref=dst,
            send_sem=sems.at[0],
            recv_sem=sems.at[1],
            device_id=device,
            device_id_type=MESH,
        ).wait_recv()

    def sum_start(at, tile):
        sum_out[at, 0] = tile
        sum_x[at, m] = tile
        for d in range(1, nm):
            send(sum_out.at[at, 0], sum_x.at[at, m], sum_x_sems.at[at, d], x_id(d))

    def sum_second(at):
        for d in range(1, nm):
            arrive(sum_x.at[at, x_peer(nm - d)], sum_x_sems.at[at, d], x_id(d))
        tile = sum_x[at, 0]
        for i in range(1, nm):
            tile = tile + sum_x[at, i]
        sum_out[at, 1] = tile
        sum_y[at, y] = tile
        for d in range(1, ny):
            send(sum_out.at[at, 1], sum_y.at[at, y], sum_y_sems.at[at, d], y_id(d))

    def sum_third(at):
        for d in range(1, ny):
            arrive(sum_y.at[at, y_peer(ny - d)], sum_y_sems.at[at, d], y_id(d))
        tile = sum_y[at, 0]
        for i in range(1, ny):
            tile = tile + sum_y[at, i]
        sum_out[at, 2] = tile
        sum_z[at, z] = tile
        for d in range(1, nz):
            send(sum_out.at[at, 2], sum_z.at[at, z], sum_z_sems.at[at, d], z_id(d))

    def sum_end(at):
        for d in range(1, nz):
            arrive(sum_z.at[at, z_peer(nz - d)], sum_z_sems.at[at, d], z_id(d))
        tile = sum_z[at, 0]
        for i in range(1, nz):
            tile = tile + sum_z[at, i]
        return jnp.sum(tile, axis=1, keepdims=True)

    def pack(lanes):
        line = lax.broadcasted_iota(jnp.int32, (8, 128), 0)
        tile = jnp.zeros((8, 128), jnp.float32)
        for i, value in enumerate(lanes):
            tile = jnp.where(line == i, jnp.broadcast_to(value, (8, 128)), tile)
        return tile

    def cell_block(ref, t):
        return ref[:, t * block : (t + 1) * block]

    def lanes_of(product):
        total = product(0)
        for t in range(1, slab):
            total = total + product(t)
        return jnp.sum(total, axis=0, keepdims=True)

    def dot_lanes(left, right):
        total = cell_block(left, 0) * cell_block(right, 0)
        for t in range(1, slab):
            total = total + cell_block(left, t) * cell_block(right, t)
        return jnp.sum(total, axis=0, keepdims=True)

    def regroup_start(at, src):
        for d in range(1, nm):
            columns = pl.ds(pl.multiple_of(x_peer(d) * width, width), width)
            send(src.at[:, columns], regroup.at[at, m], regroup_sems.at[at, d], x_id(d))
        own = pl.ds(pl.multiple_of(m * width, width), width)
        regroup[at, m] = src[:, own]

    def regroup_end(at):
        for d in range(1, nm):
            arrive(regroup.at[at, x_peer(nm - d)], regroup_sems.at[at, d], x_id(d))
        return regroup[at].reshape(modes_total, width)

    def mix_and_sum(at, vector):
        def mix(k):
            raw[at, k] = lax.dot_general(
                coupling_ref[k],
                vector,
                (((0,), (0,)), ((), ())),
                precision=lax.Precision.HIGHEST,
                preferred_element_type=jnp.float32,
            )

        third = (terms + 2) // 3
        for k in range(0, third):
            mix(k)
        sum_second(at)
        for k in range(third, min(terms, 2 * third)):
            mix(k)
        sum_third(at)
        for k in range(min(terms, 2 * third), terms):
            mix(k)
        return sum_end(at)

    def round_mixed(value):
        for k in range(terms):
            rounded = value(k).astype(jnp.bfloat16)
            for b in range(blocks_here):
                mixed[b * terms + k] = rounded[:, b * block : (b + 1) * block]

    def times(entry, blocks, at_block):
        return jnp.dot(mixed[entry], blocks[at_block], preferred_element_type=jnp.float32)

    def far_and_near(at, know_row=lambda: None, know_all=lambda: None):
        landing = x_in[at]
        x_all[at, :, entries] = jnp.zeros((nm, rows, block), jnp.float32)
        for j, (lo, hi) in enumerate(chunks):
            for place in range(lo, hi):
                entry = order_ref[place]
                x_out[at, place] = times(entry, off_ref, entry).reshape(nm, rows, block)
            for d in range(1, nm):
                send(
                    x_out.at[at, lo:hi, x_peer(d)],
                    landing.at[m, lo:hi],
                    x_sems.at[at, j, d],
                    x_id(d),
                )
            x_all[at, m, lo:hi] = x_out[at, lo:hi, m]

        def near():
            for b in range(blocks_here):
                total = times(b * terms, diag_ref, b * terms)
                for k in range(1, terms):
                    total = total + times(b * terms + k, diag_ref, b * terms + k)
                near_out[at, :, :, b * block : (b + 1) * block] = total.reshape(nm, rows, block)
            for d in range(1, nm):
                send(near_out.at[at, x_peer(d)], near_in.at[at, m], near_sems.at[at, d], x_id(d))
            near_in[at, m] = near_out[at, m]

        def hand_on(i):
            if i < len(chunks):
                lo, hi = chunks[i]
                for d in range(1, nm):
                    giver = x_peer(nm - d)
                    arrive(landing.at[giver, lo:hi], x_sems.at[at, i, d], x_id(d))
                    x_all[at, giver, lo:hi] = landing[giver, lo:hi]
            for d in list(range(1, ny)) + [0]:
                slot = i * ny + y_peer(d)
                for giver in range(nm):
                    tile = x_all[at, giver, sources[giver, 0, slot]]
                    if d:
                        y_out[at, i, d, giver] = tile
                    else:
                        y_in[at, i, y, giver] = tile
                if d:
                    send(y_out.at[at, i, d], y_in.at[at, i, y], y_sems.at[at, i, d], y_id(d))

        half = slab // 2
        up, down = (0, slice(0, half)), (1, slice(half, slab))

        def z_received(way, d, targets):
            came_from = d + 1 if way == 0 else (d - 1) % nz
            step = nz - 1 if way == 0 else 1
            held = z_in.at[at, way, turn_of[came_from], targets]
            arrive(held, z_sems.at[at, way, turn_of[came_from]], z_id(step))
            return held

        def gather(i):
            for d in range(1, ny):
                arrive(y_in.at[at, i, y_peer(ny - d)], y_sems.at[at, i, d], y_id(d))
            slot = ny * nz + i * ny + y

            def add(step, totals):
                giver_y, giver = lax.div(step, nm), lax.rem(step, nm)
                label = tables[giver_y, giver, 0, slot]
                tile = y_in[at, i, giver_y, giver]
                return tuple(total + jnp.where(label == t, tile, 0.0) for t, total in enumerate(totals))

            zero = jnp.zeros((rows, block), jnp.float32)
            totals = list(lax.fori_loop(0, ny * nm, add, (zero,) * slab))
            d = turns[i]
            middle = nz // 2
            everything = slice(0, slab)
            if d < middle:
                targets = up[1] if d + 1 == middle else everything
                held = z_received(0, d, targets)
                for t in range(targets.start, targets.stop):
                    totals[t] = totals[t] + held[t - targets.start]
            if d > middle or d == 0:
                targets = down[1] if (d - 1) % nz == middle else everything
                held = z_received(1, d, targets)
                for t in range(targets.start, targets.stop):
                    totals[t] = totals[t] + held[t - targets.start]
            if d == 0:
                for t in range(slab):
                    far_sum[at, :, t * block : (t + 1) * block] = totals[t]
                return
            for t in range(slab):
                z_out[at, i, t] = totals[t]
            if d <= middle:
                targets = up[1] if d == middle else everything
                send(z_out.at[at, i, targets], z_in.at[at, 0, i, targets], z_sems.at[at, 0, i], z_id(1))
            if d >= middle:
                targets = down[1] if d == middle else everything
                send(z_out.at[at, i, targets], z_in.at[at, 1, i, targets], z_sems.at[at, 1, i], z_id(nz - 1))

        know_row()
        lag = min(2, nz)
        for i in range(nz + lag):
            if i < nz:
                hand_on(i)
            if i == 1:
                near()
                know_all()
            if i >= lag:
                gather(i - lag)

    def complete(at):
        for d in range(1, nm):
            arrive(near_in.at[at, x_peer(nm - d)], near_sems.at[at, d], x_id(d))
        for t in range(slab):
            b = t % blocks_here
            applied[at, :, t * block : (t + 1) * block] = (
                near_in[at, t // blocks_here, :, b * block : (b + 1) * block] + far_sum[at, :, t * block : (t + 1) * block]
            )

    slots = ny * nz
    slot_of, target_of = [], []
    for e in range(entries):
        owner = owner_ref[e // terms, 0, e % terms]
        hop = lax.rem(lax.rem(owner, nz) - z + nz, nz)
        near_hop = jnp.minimum(hop, nz - hop)
        turn = jnp.maximum(nz - 2 * near_hop - jnp.where(2 * hop <= nz, 1, 0), 0)
        slot_of.append(turn * ny + lax.div(owner, nz))
        target_of.append(target_ref[e // terms, e % terms])
    place_of = []
    for e in range(entries):
        place = jnp.int32(0)
        for other in range(entries):
            if other != e:
                place = place + jnp.where(slot_of[other] < slot_of[e], 1, 0)
        place_of.append(place)
    for p in range(entries):
        entry = jnp.int32(0)
        for e in range(1, entries):
            entry = entry + jnp.where(place_of[e] == p, e, 0)
        order_ref[p] = jnp.minimum(entry, entries - 1)
    lane = lax.broadcasted_iota(jnp.int32, (1, 128), 1)
    there = jnp.zeros((1, 128), jnp.int32)
    before = jnp.zeros((1, 128), jnp.int32)
    label = jnp.full((1, 128), -1, jnp.int32)
    for e in range(entries):
        there = there + jnp.where(lane == slot_of[e], 1, 0)
        before = before + jnp.where(lane > slot_of[e], 1, 0)
        label = jnp.where(lane - slots == slot_of[e], target_of[e], label)
    table_out[...] = jnp.where(lane < slots, jnp.where(there > 0, before, entries), label)

    loads[0].wait()
    pl.semaphore_wait(barrier, len(everyone))
    sum_start(0, pack([dot_lanes(source_ref, source_ref)]))
    regroup_start(0, source_ref)
    for d in range(1, nm):
        send(table_out, tables_row.at[m], table_sems.at[0, d], x_id(d))
    tables_row[m] = table_out[...]
    loads[1].wait()
    for d in range(1, nm):
        arrive(tables_row.at[x_peer(nm - d)], table_sems.at[0, d], x_id(d))
    for d in range(1, ny):
        send(tables_row, tables_all.at[y], table_sems.at[1, d], y_id(d))
    row_copy = pltpu.make_async_copy(tables_row, sources, local_sems.at[0])
    row_copy.start()
    tables_all[y] = tables_row[...]
    sums = mix_and_sum(0, regroup_end(0))
    size = jnp.sqrt(sums[0:1])
    shrink = 1.0 / size
    round_mixed(lambda k: raw[0, k] * shrink)
    loads[2].wait()
    loads[3].wait()

    def know_row():
        row_copy.wait()

    def know_all():
        for d in range(1, ny):
            arrive(tables_all.at[y_peer(ny - d)], table_sems.at[1, d], y_id(d))
        all_copy = pltpu.make_async_copy(tables_all, tables, local_sems.at[1])
        all_copy.start()
        all_copy.wait()

    far_and_near(0, know_row, know_all)

    first, second = applied.at[0], applied.at[1]
    complete(0)
    sum_start(1, pack([dot_lanes(first, source_ref), dot_lanes(first, first)]))
    regroup_start(1, far_sum.at[0])
    far = regroup_end(1)
    sums = mix_and_sum(1, far + near_out[0].reshape(modes_total, width))
    h00 = sums[0:1] * shrink
    h10 = jnp.sqrt(jnp.maximum(sums[1:2] - h00 * h00, 0.0))
    lean = h00 * shrink
    shrink_1 = 1.0 / h10
    round_mixed(lambda k: (raw[1, k] - lean * raw[0, k]) * shrink_1)
    far_and_near(1)
    complete(1)

    def basis_0(t):
        return cell_block(source_ref, t) * shrink

    def basis_1(t):
        return (cell_block(first, t) - lean * cell_block(source_ref, t)) * shrink_1

    sum_start(
        2,
        pack(
            [
                lanes_of(lambda t: cell_block(second, t) * basis_0(t)),
                lanes_of(lambda t: cell_block(second, t) * basis_1(t)),
                lanes_of(lambda t: cell_block(second, t) * cell_block(second, t)),
                lanes_of(lambda t: basis_0(t) * basis_1(t)),
                lanes_of(lambda t: basis_1(t) * basis_1(t)),
            ]
        ),
    )
    sum_second(2)
    sum_third(2)
    sums = sum_end(2)
    h01, cross = sums[0:1], sums[3:4]
    h11 = sums[1:2] - h01 * cross
    h21 = jnp.sqrt(
        jnp.maximum(
            sums[2:3]
            - 2.0 * h01 * h01
            - 2.0 * h11 * sums[1:2]
            + h01 * h01
            + h11 * h11 * sums[4:5]
            + 2.0 * h01 * h11 * cross,
            0.0,
        )
    )

    r00 = jnp.sqrt(h00 * h00 + h10 * h10)
    cos0, sin0 = h00 / r00, h10 / r00
    g1 = -sin0 * size
    g0 = cos0 * size
    r01 = cos0 * h01 + sin0 * h11
    low = cos0 * h11 - sin0 * h01
    r11 = jnp.sqrt(low * low + h21 * h21)
    g1 = (low / r11) * g1
    y1 = g1 / r11
    y0 = (g0 - r01 * y1) / r00
    grow = size / h21
    for t in range(slab):
        v0, v1 = basis_0(t), basis_1(t)
        solution_ref[:, t * block : (t + 1) * block] = y0 * v0 + y1 * v1
        next_ref[:, t * block : (t + 1) * block] = (cell_block(second, t) - h01 * v0 - h11 * v1) * grow

    for copy in started:
        copy.wait_send()


def body(cells_y, cells_z, adjoint_source, coupling, diag_blocks, off_blocks, owner_cells, target_block):
    nm = lax.axis_size("modes")
    blocks_here, terms, block = diag_blocks.shape[:3]
    modes_total = coupling.shape[1]
    entries = terms * blocks_here
    rows = modes_total // nm
    slab = nm * blocks_here
    width = blocks_here * block
    dims = (cells_y, cells_z, nm, terms, blocks_here)
    f32, bf16 = jnp.float32, jnp.bfloat16
    chunk_count = -(-entries // cells_y)
    dma = pltpu.SemaphoreType.DMA
    vmem = pl.BlockSpec(memory_space=pltpu.VMEM)
    smem = pl.BlockSpec(memory_space=pltpu.SMEM)
    anywhere = pl.BlockSpec(memory_space=pl.ANY)
    return pl.pallas_call(
        functools.partial(kernel, dims),
        out_shape=[jax.ShapeDtypeStruct(adjoint_source.shape, f32)] * 2,
        in_specs=[smem, smem] + [anywhere] * 4,
        out_specs=[vmem, vmem],
        scratch_shapes=[
            pltpu.VMEM((rows, slab * block), f32),
            pltpu.VMEM((terms, modes_total, modes_total), f32),
            pltpu.VMEM((entries, block, block), bf16),
            pltpu.VMEM((entries, block, block), bf16),
            dma((4,)),
            pltpu.SMEM((entries,), jnp.int32),
            pltpu.VMEM((1, 128), jnp.int32),
            pltpu.VMEM((nm, 1, 128), jnp.int32),
            pltpu.VMEM((cells_y, nm, 1, 128), jnp.int32),
            pltpu.SMEM((nm, 1, 128), jnp.int32),
            pltpu.SMEM((cells_y, nm, 1, 128), jnp.int32),
            pltpu.VMEM((2, nm, rows, width), f32),
            pltpu.VMEM((2, terms, modes_total, width), f32),
            pltpu.VMEM((entries, modes_total, block), bf16),
            pltpu.VMEM((2, entries, nm, rows, block), f32),
            pltpu.VMEM((nm, entries, rows, block), f32),
            pltpu.VMEM((nm, entries, rows, block), f32),
            pltpu.VMEM((2, nm, entries + 1, rows, block), f32),
            pltpu.VMEM((2, cells_z, cells_y, nm, rows, block), f32),
            pltpu.VMEM((2, cells_z, cells_y, nm, rows, block), f32),
            pltpu.VMEM((2, cells_z, slab, rows, block), f32),
            pltpu.VMEM((2, 2, cells_z, slab, rows, block), f32),
            pltpu.VMEM((2, nm, rows, width), f32),
            pltpu.VMEM((2, nm, rows, width), f32),
            pltpu.VMEM((2, rows, slab * block), f32),
            pltpu.VMEM((2, rows, slab * block), f32),
            pltpu.VMEM((3, 3, 8, 128), f32),
            pltpu.VMEM((3, nm, 8, 128), f32),
            pltpu.VMEM((3, cells_y, 8, 128), f32),
            pltpu.VMEM((3, cells_z, 8, 128), f32),
            dma((2, max(nm, cells_y), 2)),
            dma((2,)),
            dma((2, nm, 2)),
            dma((2, chunk_count, nm, 2)),
            dma((2, cells_z, cells_y, 2)),
            dma((2, 2, cells_z, 2)),
            dma((2, nm, 2)),
            dma((3, nm, 2)),
            dma((3, cells_y, 2)),
            dma((3, cells_z, 2)),
        ],
        compiler_params=pltpu.CompilerParams(
            collective_id=0, has_side_effects=True, vmem_limit_bytes=62 * 1024 * 1024
        ),
    )(
        owner_cells.transpose(0, 2, 1),
        target_block,
        adjoint_source,
        coupling,
        diag_blocks.reshape(entries, block, block),
        off_blocks.reshape(entries, block, block),
    )


def solution(mesh, cells_z=8):
    cells_y = mesh.shape["cells"] // cells_z
    placed = (
        P("modes", "cells"),
        P(),
        P(("cells", "modes"), None, None, None),
        P(("cells", "modes"), None, None, None),
        P(("cells", "modes"), None, None),
        P(("cells", "modes"), None),
    )
    return jax.shard_map(
        functools.partial(body, cells_y, cells_z),
        mesh=mesh,
        in_specs=placed,
        out_specs=(P("modes", "cells"), P("modes", "cells")),
        check_vma=False,
    )
```

```python
import functools

import jax
import jax.numpy as jnp
from jax import lax
from jax.experimental import pallas as pl
from jax.experimental.pallas import tpu as pltpu
from jax.sharding import PartitionSpec as P

MESH = pl.DeviceIdType.MESH


def far_first(count):
    return sorted(range(count), key=lambda step: (-min(step, count - step), step))


def kernel(
    dims,
    owner_ref,
    target_ref,
    source_hbm,
    coupling_hbm,
    diag_hbm,
    off_hbm,
    solution_ref,
    next_ref,
    source_ref,
    coupling_ref,
    diag_ref,
    off_ref,
    load_sems,
    order_ref,
    table_out,
    tables_row,
    tables_all,
    sources,
    tables,
    regroup,
    raw,
    mixed,
    x_out,
    x_in_0,
    x_in_1,
    x_all,
    y_out,
    y_in,
    z_out,
    z_in,
    near_out,
    near_in,
    far_sum,
    applied,
    sum_out,
    sum_x,
    sum_y,
    sum_z,
    table_sems,
    local_sems,
    regroup_sems,
    x_sems,
    y_sems,
    z_sems,
    near_sems,
    sum_x_sems,
    sum_y_sems,
    sum_z_sems,
):
    ny, nz, nm, terms, blocks_here = dims
    modes_total, block = coupling_ref.shape[1], off_ref.shape[-1]
    rows = modes_total // nm
    entries = terms * blocks_here
    slab = nm * blocks_here
    width = blocks_here * block
    turns = far_first(nz)
    turn_of = {d: i for i, d in enumerate(turns)}
    cuts = [min(entries, ny * step) for step in range(nz + 1)]
    chunks = [(lo, hi) for lo, hi in zip(cuts[:-1], cuts[1:]) if hi > lo]
    x_in = (x_in_0, x_in_1)

    c = lax.axis_index("cells")
    m = lax.axis_index("modes")
    y, z = lax.div(c, nz), lax.rem(c, nz)

    def x_peer(d):
        return lax.rem(m + d, nm)

    def y_peer(d):
        return lax.rem(y + d, ny)

    def z_peer(d):
        return lax.rem(z + d, nz)

    def x_id(d):
        return (c, x_peer(d))

    def y_id(d):
        return (y_peer(d) * nz + z, m)

    def z_id(d):
        return (y * nz + z_peer(d), m)

    everyone = (
        [x_id(d) for d in range(1, nm)]
        + [y_id(d) for d in range(1, ny)]
        + [z_id(d) for d in range(1, nz)]
    )
    barrier = pltpu.get_barrier_semaphore()
    for device in everyone:
        pl.semaphore_signal(barrier, inc=1, device_id=device, device_id_type=MESH)
    loads = [
        pltpu.make_async_copy(src, dst, load_sems.at[i])
        for i, (src, dst) in enumerate(
            [
                (source_hbm, source_ref),
                (coupling_hbm, coupling_ref),
                (off_hbm, off_ref),
                (diag_hbm, diag_ref),
            ]
        )
    ]
    for load in loads:
        load.start()

    started = []

    def send(src, dst, sems, device):
        copy = pltpu.make_async_remote_copy(
            src_ref=src,
            dst_ref=dst,
            send_sem=sems.at[0],
            recv_sem=sems.at[1],
            device_id=device,
            device_id_type=MESH,
        )
        copy.start()
        started.append(copy)

    def arrive(dst, sems, device):
        pltpu.make_async_remote_copy(
            src_ref=dst,
            dst_ref=dst,
            send_sem=sems.at[0],
            recv_sem=sems.at[1],
            device_id=device,
            device_id_type=MESH,
        ).wait_recv()

    def sum_start(at, tile):
        sum_out[at, 0] = tile
        sum_x[at, m] = tile
        for d in range(1, nm):
            send(sum_out.at[at, 0], sum_x.at[at, m], sum_x_sems.at[at, d], x_id(d))

    def sum_second(at):
        for d in range(1, nm):
            arrive(sum_x.at[at, x_peer(nm - d)], sum_x_sems.at[at, d], x_id(d))
        tile = sum_x[at, 0]
        for i in range(1, nm):
            tile = tile + sum_x[at, i]
        sum_out[at, 1] = tile
        sum_y[at, y] = tile
        for d in range(1, ny):
            send(sum_out.at[at, 1], sum_y.at[at, y], sum_y_sems.at[at, d], y_id(d))

    def sum_third(at):
        for d in range(1, ny):
            arrive(sum_y.at[at, y_peer(ny - d)], sum_y_sems.at[at, d], y_id(d))
        tile = sum_y[at, 0]
        for i in range(1, ny):
            tile = tile + sum_y[at, i]
        sum_out[at, 2] = tile
        sum_z[at, z] = tile
        for d in range(1, nz):
            send(sum_out.at[at, 2], sum_z.at[at, z], sum_z_sems.at[at, d], z_id(d))

    def sum_end(at):
        for d in range(1, nz):
            arrive(sum_z.at[at, z_peer(nz - d)], sum_z_sems.at[at, d], z_id(d))
        tile = sum_z[at, 0]
        for i in range(1, nz):
            tile = tile + sum_z[at, i]
        return jnp.sum(tile, axis=1, keepdims=True)

    def pack(lanes):
        line = lax.broadcasted_iota(jnp.int32, (8, 128), 0)
        tile = jnp.zeros((8, 128), jnp.float32)
        for i, value in enumerate(lanes):
            tile = jnp.where(line == i, jnp.broadcast_to(value, (8, 128)), tile)
        return tile

    def cell_block(ref, t):
        return ref[:, t * block : (t + 1) * block]

    def lanes_of(product):
        total = product(0)
        for t in range(1, slab):
            total = total + product(t)
        return jnp.sum(total, axis=0, keepdims=True)

    def dot_lanes(left, right):
        total = cell_block(left, 0) * cell_block(right, 0)
        for t in range(1, slab):
            total = total + cell_block(left, t) * cell_block(right, t)
        return jnp.sum(total, axis=0, keepdims=True)

    def regroup_start(at, src):
        for d in range(1, nm):
            columns = pl.ds(pl.multiple_of(x_peer(d) * width, width), width)
            send(src.at[:, columns], regroup.at[at, m], regroup_sems.at[at, d], x_id(d))
        own = pl.ds(pl.multiple_of(m * width, width), width)
        regroup[at, m] = src[:, own]

    def regroup_end(at):
        for d in range(1, nm):
            arrive(regroup.at[at, x_peer(nm - d)], regroup_sems.at[at, d], x_id(d))
        return regroup[at].reshape(modes_total, width)

    def mix_and_sum(at, vector):
        def mix(k):
            raw[at, k] = lax.dot_general(
                coupling_ref[k],
                vector,
                (((0,), (0,)), ((), ())),
                precision=lax.Precision.HIGHEST,
                preferred_element_type=jnp.float32,
            )

        half = terms // 2
        sum_second(at)
        for k in range(0, half):
            mix(k)
        sum_third(at)
        for k in range(half, terms):
            mix(k)
        return sum_end(at)

    def round_mixed(value):
        for k in range(terms):
            rounded = value(k).astype(jnp.bfloat16)
            for b in range(blocks_here):
                mixed[b * terms + k] = rounded[:, b * block : (b + 1) * block]

    def times(entry, blocks, at_block):
        return jnp.dot(mixed[entry], blocks[at_block], preferred_element_type=jnp.float32)

    def far_and_near(at, know_row=lambda: None, know_all=lambda: None):
        landing = x_in[at]
        x_all[at, :, entries] = jnp.zeros((nm, rows, block), jnp.float32)
        for j, (lo, hi) in enumerate(chunks):
            for place in range(lo, hi):
                entry = order_ref[place]
                x_out[at, place] = times(entry, off_ref, entry).reshape(nm, rows, block)
            for d in range(1, nm):
                send(
                    x_out.at[at, lo:hi, x_peer(d)],
                    landing.at[m, lo:hi],
                    x_sems.at[at, j, d],
                    x_id(d),
                )
            x_all[at, m, lo:hi] = x_out[at, lo:hi, m]

        def near():
            for b in range(blocks_here):
                total = times(b * terms, diag_ref, b * terms)
                for k in range(1, terms):
                    total = total + times(b * terms + k, diag_ref, b * terms + k)
                near_out[at, :, :, b * block : (b + 1) * block] = total.reshape(nm, rows, block)
            for d in range(1, nm):
                send(near_out.at[at, x_peer(d)], near_in.at[at, m], near_sems.at[at, d], x_id(d))
            near_in[at, m] = near_out[at, m]

        def hand_on(i):
            if i < len(chunks):
                lo, hi = chunks[i]
                for d in range(1, nm):
                    giver = x_peer(nm - d)
                    arrive(landing.at[giver, lo:hi], x_sems.at[at, i, d], x_id(d))
                    x_all[at, giver, lo:hi] = landing[giver, lo:hi]
            for d in list(range(1, ny)) + [0]:
                slot = i * ny + y_peer(d)
                for giver in range(nm):
                    tile = x_all[at, giver, sources[giver, 0, slot]]
                    if d:
                        y_out[at, i, d, giver] = tile
                    else:
                        y_in[at, i, y, giver] = tile
                if d:
                    send(y_out.at[at, i, d], y_in.at[at, i, y], y_sems.at[at, i, d], y_id(d))

        half = slab // 2
        up, down = (0, slice(0, half)), (1, slice(half, slab))

        def z_received(way, d, targets):
            came_from = d + 1 if way == 0 else (d - 1) % nz
            step = nz - 1 if way == 0 else 1
            held = z_in.at[at, way, turn_of[came_from], targets]
            arrive(held, z_sems.at[at, way, turn_of[came_from]], z_id(step))
            return held

        def gather(i):
            for d in range(1, ny):
                arrive(y_in.at[at, i, y_peer(ny - d)], y_sems.at[at, i, d], y_id(d))
            slot = ny * nz + i * ny + y

            def add(step, totals):
                giver_y, giver = lax.div(step, nm), lax.rem(step, nm)
                label = tables[giver_y, giver, 0, slot]
                tile = y_in[at, i, giver_y, giver]
                return tuple(total + jnp.where(label == t, tile, 0.0) for t, total in enumerate(totals))

            zero = jnp.zeros((rows, block), jnp.float32)
            totals = list(lax.fori_loop(0, ny * nm, add, (zero,) * slab, unroll=4))
            d = turns[i]
            middle = nz // 2
            everything = slice(0, slab)
            if d < middle:
                targets = up[1] if d + 1 == middle else everything
                held = z_received(0, d, targets)
                for t in range(targets.start, targets.stop):
                    totals[t] = totals[t] + held[t - targets.start]
            if d > middle or d == 0:
                targets = down[1] if (d - 1) % nz == middle else everything
                held = z_received(1, d, targets)
                for t in range(targets.start, targets.stop):
                    totals[t] = totals[t] + held[t - targets.start]
            if d == 0:
                for t in range(slab):
                    far_sum[at, :, t * block : (t + 1) * block] = totals[t]
                return
            for t in range(slab):
                z_out[at, i, t] = totals[t]
            if d <= middle:
                targets = up[1] if d == middle else everything
                send(z_out.at[at, i, targets], z_in.at[at, 0, i, targets], z_sems.at[at, 0, i], z_id(1))
            if d >= middle:
                targets = down[1] if d == middle else everything
                send(z_out.at[at, i, targets], z_in.at[at, 1, i, targets], z_sems.at[at, 1, i], z_id(nz - 1))

        know_row()
        lag = min(2, nz)
        for i in range(nz + lag):
            if i < nz:
                hand_on(i)
            if i == 1:
                near()
                know_all()
            if i >= lag:
                gather(i - lag)

    def complete(at):
        for d in range(1, nm):
            arrive(near_in.at[at, x_peer(nm - d)], near_sems.at[at, d], x_id(d))
        for t in range(slab):
            b = t % blocks_here
            applied[at, :, t * block : (t + 1) * block] = (
                near_in[at, t // blocks_here, :, b * block : (b + 1) * block] + far_sum[at, :, t * block : (t + 1) * block]
            )

    slots = ny * nz
    slot_of, target_of = [], []
    for e in range(entries):
        owner = owner_ref[e // terms, 0, e % terms]
        hop = lax.rem(lax.rem(owner, nz) - z + nz, nz)
        near_hop = jnp.minimum(hop, nz - hop)
        turn = jnp.maximum(nz - 2 * near_hop - jnp.where(2 * hop <= nz, 1, 0), 0)
        slot_of.append(turn * ny + lax.div(owner, nz))
        target_of.append(target_ref[e // terms, e % terms])
    place_of = []
    for e in range(entries):
        place = jnp.int32(0)
        for other in range(entries):
            if other != e:
                place = place + jnp.where(slot_of[other] < slot_of[e], 1, 0)
        place_of.append(place)
    for p in range(entries):
        entry = jnp.int32(0)
        for e in range(1, entries):
            entry = entry + jnp.where(place_of[e] == p, e, 0)
        order_ref[p] = jnp.minimum(entry, entries - 1)
    lane = lax.broadcasted_iota(jnp.int32, (1, 128), 1)
    there = jnp.zeros((1, 128), jnp.int32)
    before = jnp.zeros((1, 128), jnp.int32)
    label = jnp.full((1, 128), -1, jnp.int32)
    for e in range(entries):
        there = there + jnp.where(lane == slot_of[e], 1, 0)
        before = before + jnp.where(lane > slot_of[e], 1, 0)
        label = jnp.where(lane - slots == slot_of[e], target_of[e], label)
    table_out[...] = jnp.where(lane < slots, jnp.where(there > 0, before, entries), label)

    loads[0].wait()
    pl.semaphore_wait(barrier, len(everyone))
    sum_start(0, pack([dot_lanes(source_ref, source_ref)]))
    regroup_start(0, source_ref)
    for d in range(1, nm):
        send(table_out, tables_row.at[m], table_sems.at[0, d], x_id(d))
    tables_row[m] = table_out[...]
    loads[1].wait()
    for d in range(1, nm):
        arrive(tables_row.at[x_peer(nm - d)], table_sems.at[0, d], x_id(d))
    for d in range(1, ny):
        send(tables_row, tables_all.at[y], table_sems.at[1, d], y_id(d))
    row_copy = pltpu.make_async_copy(tables_row, sources, local_sems.at[0])
    row_copy.start()
    tables_all[y] = tables_row[...]
    sums = mix_and_sum(0, regroup_end(0))
    size = jnp.sqrt(sums[0:1])
    shrink = 1.0 / size
    round_mixed(lambda k: raw[0, k] * shrink)
    loads[2].wait()
    loads[3].wait()

    def know_row():
        row_copy.wait()

    def know_all():
        for d in range(1, ny):
            arrive(tables_all.at[y_peer(ny - d)], table_sems.at[1, d], y_id(d))
        all_copy = pltpu.make_async_copy(tables_all, tables, local_sems.at[1])
        all_copy.start()
        all_copy.wait()

    far_and_near(0, know_row, know_all)

    first, second = applied.at[0], applied.at[1]
    complete(0)
    sum_start(1, pack([dot_lanes(first, source_ref), dot_lanes(first, first)]))
    regroup_start(1, far_sum.at[0])
    far = regroup_end(1)
    sums = mix_and_sum(1, far + near_out[0].reshape(modes_total, width))
    h00 = sums[0:1] * shrink
    h10 = jnp.sqrt(jnp.maximum(sums[1:2] - h00 * h00, 0.0))
    lean = h00 * shrink
    shrink_1 = 1.0 / h10
    round_mixed(lambda k: (raw[1, k] - lean * raw[0, k]) * shrink_1)
    far_and_near(1)
    complete(1)

    def basis_0(t):
        return cell_block(source_ref, t) * shrink

    def basis_1(t):
        return (cell_block(first, t) - lean * cell_block(source_ref, t)) * shrink_1

    sum_start(
        2,
        pack(
            [
                lanes_of(lambda t: cell_block(second, t) * basis_0(t)),
                lanes_of(lambda t: cell_block(second, t) * basis_1(t)),
                lanes_of(lambda t: cell_block(second, t) * cell_block(second, t)),
                lanes_of(lambda t: basis_0(t) * basis_1(t)),
                lanes_of(lambda t: basis_1(t) * basis_1(t)),
            ]
        ),
    )
    sum_second(2)
    sum_third(2)
    sums = sum_end(2)
    h01, cross = sums[0:1], sums[3:4]
    h11 = sums[1:2] - h01 * cross
    h21 = jnp.sqrt(
        jnp.maximum(
            sums[2:3]
            - 2.0 * h01 * h01
            - 2.0 * h11 * sums[1:2]
            + h01 * h01
            + h11 * h11 * sums[4:5]
            + 2.0 * h01 * h11 * cross,
            0.0,
        )
    )

    r00 = jnp.sqrt(h00 * h00 + h10 * h10)
    cos0, sin0 = h00 / r00, h10 / r00
    g1 = -sin0 * size
    g0 = cos0 * size
    r01 = cos0 * h01 + sin0 * h11
    low = cos0 * h11 - sin0 * h01
    r11 = jnp.sqrt(low * low + h21 * h21)
    g1 = (low / r11) * g1
    y1 = g1 / r11
    y0 = (g0 - r01 * y1) / r00
    grow = size / h21
    for t in range(slab):
        v0, v1 = basis_0(t), basis_1(t)
        solution_ref[:, t * block : (t + 1) * block] = y0 * v0 + y1 * v1
        next_ref[:, t * block : (t + 1) * block] = (cell_block(second, t) - h01 * v0 - h11 * v1) * grow

    for copy in started:
        copy.wait_send()


def body(cells_y, cells_z, adjoint_source, coupling, diag_blocks, off_blocks, owner_cells, target_block):
    nm = lax.axis_size("modes")
    blocks_here, terms, block = diag_blocks.shape[:3]
    modes_total = coupling.shape[1]
    entries = terms * blocks_here
    rows = modes_total // nm
    slab = nm * blocks_here
    width = blocks_here * block
    dims = (cells_y, cells_z, nm, terms, blocks_here)
    f32, bf16 = jnp.float32, jnp.bfloat16
    chunk_count = -(-entries // cells_y)
    dma = pltpu.SemaphoreType.DMA
    vmem = pl.BlockSpec(memory_space=pltpu.VMEM)
    smem = pl.BlockSpec(memory_space=pltpu.SMEM)
    anywhere = pl.BlockSpec(memory_space=pl.ANY)
    return pl.pallas_call(
        functools.partial(kernel, dims),
        out_shape=[jax.ShapeDtypeStruct(adjoint_source.shape, f32)] * 2,
        in_specs=[smem, smem] + [anywhere] * 4,
        out_specs=[vmem, vmem],
        scratch_shapes=[
            pltpu.VMEM((rows, slab * block), f32),
            pltpu.VMEM((terms, modes_total, modes_total), f32),
            pltpu.VMEM((entries, block, block), bf16),
            pltpu.VMEM((entries, block, block), bf16),
            dma((4,)),
            pltpu.SMEM((entries,), jnp.int32),
            pltpu.VMEM((1, 128), jnp.int32),
            pltpu.VMEM((nm, 1, 128), jnp.int32),
            pltpu.VMEM((cells_y, nm, 1, 128), jnp.int32),
            pltpu.SMEM((nm, 1, 128), jnp.int32),
            pltpu.SMEM((cells_y, nm, 1, 128), jnp.int32),
            pltpu.VMEM((2, nm, rows, width), f32),
            pltpu.VMEM((2, terms, modes_total, width), f32),
            pltpu.VMEM((entries, modes_total, block), bf16),
            pltpu.VMEM((2, entries, nm, rows, block), f32),
            pltpu.VMEM((nm, entries, rows, block), f32),
            pltpu.VMEM((nm, entries, rows, block), f32),
            pltpu.VMEM((2, nm, entries + 1, rows, block), f32),
            pltpu.VMEM((2, cells_z, cells_y, nm, rows, block), f32),
            pltpu.VMEM((2, cells_z, cells_y, nm, rows, block), f32),
            pltpu.VMEM((2, cells_z, slab, rows, block), f32),
            pltpu.VMEM((2, 2, cells_z, slab, rows, block), f32),
            pltpu.VMEM((2, nm, rows, width), f32),
            pltpu.VMEM((2, nm, rows, width), f32),
            pltpu.VMEM((2, rows, slab * block), f32),
            pltpu.VMEM((2, rows, slab * block), f32),
            pltpu.VMEM((3, 3, 8, 128), f32),
            pltpu.VMEM((3, nm, 8, 128), f32),
            pltpu.VMEM((3, cells_y, 8, 128), f32),
            pltpu.VMEM((3, cells_z, 8, 128), f32),
            dma((2, max(nm, cells_y), 2)),
            dma((2,)),
            dma((2, nm, 2)),
            dma((2, chunk_count, nm, 2)),
            dma((2, cells_z, cells_y, 2)),
            dma((2, 2, cells_z, 2)),
            dma((2, nm, 2)),
            dma((3, nm, 2)),
            dma((3, cells_y, 2)),
            dma((3, cells_z, 2)),
        ],
        compiler_params=pltpu.CompilerParams(
            collective_id=0, has_side_effects=True, vmem_limit_bytes=62 * 1024 * 1024
        ),
    )(
        owner_cells.transpose(0, 2, 1),
        target_block,
        adjoint_source,
        coupling,
        diag_blocks.reshape(entries, block, block),
        off_blocks.reshape(entries, block, block),
    )


def solution(mesh, cells_z=8):
    cells_y = mesh.shape["cells"] // cells_z
    placed = (
        P("modes", "cells"),
        P(),
        P(("cells", "modes"), None, None, None),
        P(("cells", "modes"), None, None, None),
        P(("cells", "modes"), None, None),
        P(("cells", "modes"), None),
    )
    return jax.shard_map(
        functools.partial(body, cells_y, cells_z),
        mesh=mesh,
        in_specs=placed,
        out_specs=(P("modes", "cells"), P("modes", "cells")),
        check_vma=False,
    )
```

```python
import functools

import jax
import jax.numpy as jnp
from jax import lax
from jax.experimental import pallas as pl
from jax.experimental.pallas import tpu as pltpu
from jax.sharding import PartitionSpec as P

MESH = pl.DeviceIdType.MESH


def far_first(count):
    return sorted(range(count), key=lambda step: (-min(step, count - step), step))


def kernel(
    dims,
    owner_ref,
    target_ref,
    source_hbm,
    coupling_hbm,
    diag_hbm,
    off_hbm,
    solution_ref,
    next_ref,
    source_ref,
    coupling_ref,
    diag_ref,
    off_ref,
    load_sems,
    order_ref,
    table_out,
    tables_row,
    tables_all,
    sources,
    tables,
    regroup,
    raw,
    mixed,
    x_out,
    x_in_0,
    x_in_1,
    x_all,
    y_out,
    y_in,
    z_out,
    z_in,
    near_out,
    near_in,
    far_sum,
    applied,
    sum_out,
    sum_x,
    sum_y,
    sum_z,
    table_sems,
    local_sems,
    regroup_sems,
    x_sems,
    y_sems,
    z_sems,
    near_sems,
    sum_x_sems,
    sum_y_sems,
    sum_z_sems,
):
    ny, nz, nm, terms, blocks_here = dims
    modes_total, block = coupling_ref.shape[1], off_ref.shape[-1]
    rows = modes_total // nm
    entries = terms * blocks_here
    slab = nm * blocks_here
    width = blocks_here * block
    turns = far_first(nz)
    turn_of = {d: i for i, d in enumerate(turns)}
    cuts = [min(entries, ny * step) for step in range(nz + 1)]
    chunks = [(lo, hi) for lo, hi in zip(cuts[:-1], cuts[1:]) if hi > lo]
    x_in = (x_in_0, x_in_1)

    c = lax.axis_index("cells")
    m = lax.axis_index("modes")
    y, z = lax.div(c, nz), lax.rem(c, nz)

    def x_peer(d):
        return lax.rem(m + d, nm)

    def y_peer(d):
        return lax.rem(y + d, ny)

    def z_peer(d):
        return lax.rem(z + d, nz)

    def x_id(d):
        return (c, x_peer(d))

    def y_id(d):
        return (y_peer(d) * nz + z, m)

    def z_id(d):
        return (y * nz + z_peer(d), m)

    everyone = (
        [x_id(d) for d in range(1, nm)]
        + [y_id(d) for d in range(1, ny)]
        + [z_id(d) for d in range(1, nz)]
    )
    barrier = pltpu.get_barrier_semaphore()
    for device in everyone:
        pl.semaphore_signal(barrier, inc=1, device_id=device, device_id_type=MESH)
    loads = [
        pltpu.make_async_copy(src, dst, load_sems.at[i])
        for i, (src, dst) in enumerate(
            [
                (source_hbm, source_ref),
                (coupling_hbm, coupling_ref),
                (off_hbm, off_ref),
                (diag_hbm, diag_ref),
            ]
        )
    ]
    for load in loads:
        load.start()

    started = []

    def send(src, dst, sems, device):
        copy = pltpu.make_async_remote_copy(
            src_ref=src,
            dst_ref=dst,
            send_sem=sems.at[0],
            recv_sem=sems.at[1],
            device_id=device,
            device_id_type=MESH,
        )
        copy.start()
        started.append(copy)

    def arrive(dst, sems, device):
        pltpu.make_async_remote_copy(
            src_ref=dst,
            dst_ref=dst,
            send_sem=sems.at[0],
            recv_sem=sems.at[1],
            device_id=device,
            device_id_type=MESH,
        ).wait_recv()

    def sum_start(at, tile):
        sum_out[at, 0] = tile
        sum_x[at, m] = tile
        for d in range(1, nm):
            send(sum_out.at[at, 0], sum_x.at[at, m], sum_x_sems.at[at, d], x_id(d))

    def sum_second(at):
        for d in range(1, nm):
            arrive(sum_x.at[at, x_peer(nm - d)], sum_x_sems.at[at, d], x_id(d))
        tile = sum_x[at, 0]
        for i in range(1, nm):
            tile = tile + sum_x[at, i]
        sum_out[at, 1] = tile
        sum_y[at, y] = tile
        for d in range(1, ny):
            send(sum_out.at[at, 1], sum_y.at[at, y], sum_y_sems.at[at, d], y_id(d))

    def sum_third(at):
        for d in range(1, ny):
            arrive(sum_y.at[at, y_peer(ny - d)], sum_y_sems.at[at, d], y_id(d))
        tile = sum_y[at, 0]
        for i in range(1, ny):
            tile = tile + sum_y[at, i]
        sum_out[at, 2] = tile
        sum_z[at, z] = tile
        for d in range(1, nz):
            send(sum_out.at[at, 2], sum_z.at[at, z], sum_z_sems.at[at, d], z_id(d))

    def sum_end(at):
        for d in range(1, nz):
            arrive(sum_z.at[at, z_peer(nz - d)], sum_z_sems.at[at, d], z_id(d))
        tile = sum_z[at, 0]
        for i in range(1, nz):
            tile = tile + sum_z[at, i]
        return jnp.sum(tile, axis=1, keepdims=True)

    def pack(lanes):
        line = lax.broadcasted_iota(jnp.int32, (8, 128), 0)
        tile = jnp.zeros((8, 128), jnp.float32)
        for i, value in enumerate(lanes):
            tile = jnp.where(line == i, jnp.broadcast_to(value, (8, 128)), tile)
        return tile

    def cell_block(ref, t):
        return ref[:, t * block : (t + 1) * block]

    def lanes_of(product):
        total = product(0)
        for t in range(1, slab):
            total = total + product(t)
        return jnp.sum(total, axis=0, keepdims=True)

    def dot_lanes(left, right):
        total = cell_block(left, 0) * cell_block(right, 0)
        for t in range(1, slab):
            total = total + cell_block(left, t) * cell_block(right, t)
        return jnp.sum(total, axis=0, keepdims=True)

    def regroup_start(at, src):
        for d in range(1, nm):
            columns = pl.ds(pl.multiple_of(x_peer(d) * width, width), width)
            send(src.at[:, columns], regroup.at[at, m], regroup_sems.at[at, d], x_id(d))
        own = pl.ds(pl.multiple_of(m * width, width), width)
        regroup[at, m] = src[:, own]

    def regroup_end(at):
        for d in range(1, nm):
            arrive(regroup.at[at, x_peer(nm - d)], regroup_sems.at[at, d], x_id(d))
        return regroup[at].reshape(modes_total, width)

    def mix_and_sum(at, vector):
        def mix(k):
            raw[at, k] = lax.dot_general(
                coupling_ref[k],
                vector,
                (((0,), (0,)), ((), ())),
                precision=lax.Precision.HIGHEST,
                preferred_element_type=jnp.float32,
            )

        half = terms // 2
        for k in range(0, half):
            mix(k)
        sum_third(at)
        for k in range(half, terms):
            mix(k)
        return sum_end(at)

    def round_mixed(value):
        for k in range(terms):
            rounded = value(k).astype(jnp.bfloat16)
            for b in range(blocks_here):
                mixed[b * terms + k] = rounded[:, b * block : (b + 1) * block]

    def times(entry, blocks, at_block):
        return jnp.dot(mixed[entry], blocks[at_block], preferred_element_type=jnp.float32)

    def far_and_near(at, know_row=lambda: None, know_all=lambda: None):
        landing = x_in[at]
        x_all[at, :, entries] = jnp.zeros((nm, rows, block), jnp.float32)
        for j, (lo, hi) in enumerate(chunks):
            for place in range(lo, hi):
                entry = order_ref[place]
                x_out[at, place] = times(entry, off_ref, entry).reshape(nm, rows, block)
            for d in range(1, nm):
                send(
                    x_out.at[at, lo:hi, x_peer(d)],
                    landing.at[m, lo:hi],
                    x_sems.at[at, j, d],
                    x_id(d),
                )
            x_all[at, m, lo:hi] = x_out[at, lo:hi, m]

        def near():
            for b in range(blocks_here):
                total = times(b * terms, diag_ref, b * terms)
                for k in range(1, terms):
                    total = total + times(b * terms + k, diag_ref, b * terms + k)
                near_out[at, :, :, b * block : (b + 1) * block] = total.reshape(nm, rows, block)
            for d in range(1, nm):
                send(near_out.at[at, x_peer(d)], near_in.at[at, m], near_sems.at[at, d], x_id(d))
            near_in[at, m] = near_out[at, m]

        def hand_on(i):
            if i < len(chunks):
                lo, hi = chunks[i]
                for d in range(1, nm):
                    giver = x_peer(nm - d)
                    arrive(landing.at[giver, lo:hi], x_sems.at[at, i, d], x_id(d))
                    x_all[at, giver, lo:hi] = landing[giver, lo:hi]
            for d in list(range(1, ny)) + [0]:
                slot = i * ny + y_peer(d)
                for giver in range(nm):
                    tile = x_all[at, giver, sources[giver, 0, slot]]
                    if d:
                        y_out[at, i, d, giver] = tile
                    else:
                        y_in[at, i, y, giver] = tile
                if d:
                    send(y_out.at[at, i, d], y_in.at[at, i, y], y_sems.at[at, i, d], y_id(d))

        half = slab // 2
        up, down = (0, slice(0, half)), (1, slice(half, slab))

        def z_received(way, d, targets):
            came_from = d + 1 if way == 0 else (d - 1) % nz
            step = nz - 1 if way == 0 else 1
            held = z_in.at[at, way, turn_of[came_from], targets]
            arrive(held, z_sems.at[at, way, turn_of[came_from]], z_id(step))
            return held

        def gather(i):
            for d in range(1, ny):
                arrive(y_in.at[at, i, y_peer(ny - d)], y_sems.at[at, i, d], y_id(d))
            slot = ny * nz + i * ny + y

            def add(step, totals):
                giver_y, giver = lax.div(step, nm), lax.rem(step, nm)
                label = tables[giver_y, giver, 0, slot]
                tile = y_in[at, i, giver_y, giver]
                return tuple(total + jnp.where(label == t, tile, 0.0) for t, total in enumerate(totals))

            zero = jnp.zeros((rows, block), jnp.float32)
            totals = list(lax.fori_loop(0, ny * nm, add, (zero,) * slab, unroll=4))
            d = turns[i]
            middle = nz // 2
            everything = slice(0, slab)
            if d < middle:
                targets = up[1] if d + 1 == middle else everything
                held = z_received(0, d, targets)
                for t in range(targets.start, targets.stop):
                    totals[t] = totals[t] + held[t - targets.start]
            if d > middle or d == 0:
                targets = down[1] if (d - 1) % nz == middle else everything
                held = z_received(1, d, targets)
                for t in range(targets.start, targets.stop):
                    totals[t] = totals[t] + held[t - targets.start]
            if d == 0:
                for t in range(slab):
                    far_sum[at, :, t * block : (t + 1) * block] = totals[t]
                return
            for t in range(slab):
                z_out[at, i, t] = totals[t]
            if d <= middle:
                targets = up[1] if d == middle else everything
                send(z_out.at[at, i, targets], z_in.at[at, 0, i, targets], z_sems.at[at, 0, i], z_id(1))
            if d >= middle:
                targets = down[1] if d == middle else everything
                send(z_out.at[at, i, targets], z_in.at[at, 1, i, targets], z_sems.at[at, 1, i], z_id(nz - 1))

        know_row()
        lag = min(2, nz)
        for i in range(nz + lag):
            if i < nz:
                hand_on(i)
            if i == 1:
                near()
                know_all()
            if i >= lag:
                gather(i - lag)

    def complete(at):
        for d in range(1, nm):
            arrive(near_in.at[at, x_peer(nm - d)], near_sems.at[at, d], x_id(d))
        for t in range(slab):
            b = t % blocks_here
            applied[at, :, t * block : (t + 1) * block] = (
                near_in[at, t // blocks_here, :, b * block : (b + 1) * block] + far_sum[at, :, t * block : (t + 1) * block]
            )

    slots = ny * nz
    slot_of, target_of = [], []
    for e in range(entries):
        owner = owner_ref[e // terms, 0, e % terms]
        hop = lax.rem(lax.rem(owner, nz) - z + nz, nz)
        near_hop = jnp.minimum(hop, nz - hop)
        turn = jnp.maximum(nz - 2 * near_hop - jnp.where(2 * hop <= nz, 1, 0), 0)
        slot_of.append(turn * ny + lax.div(owner, nz))
        target_of.append(target_ref[e // terms, e % terms])
    place_of = []
    for e in range(entries):
        place = jnp.int32(0)
        for other in range(entries):
            if other != e:
                place = place + jnp.where(slot_of[other] < slot_of[e], 1, 0)
        place_of.append(place)
    for p in range(entries):
        entry = jnp.int32(0)
        for e in range(1, entries):
            entry = entry + jnp.where(place_of[e] == p, e, 0)
        order_ref[p] = jnp.minimum(entry, entries - 1)
    lane = lax.broadcasted_iota(jnp.int32, (1, 128), 1)
    there = jnp.zeros((1, 128), jnp.int32)
    before = jnp.zeros((1, 128), jnp.int32)
    label = jnp.full((1, 128), -1, jnp.int32)
    for e in range(entries):
        there = there + jnp.where(lane == slot_of[e], 1, 0)
        before = before + jnp.where(lane > slot_of[e], 1, 0)
        label = jnp.where(lane - slots == slot_of[e], target_of[e], label)
    table_out[...] = jnp.where(lane < slots, jnp.where(there > 0, before, entries), label)

    loads[0].wait()
    pl.semaphore_wait(barrier, len(everyone))
    sum_start(0, pack([dot_lanes(source_ref, source_ref)]))
    regroup_start(0, source_ref)
    for d in range(1, nm):
        send(table_out, tables_row.at[m], table_sems.at[0, d], x_id(d))
    tables_row[m] = table_out[...]
    loads[1].wait()
    sum_second(0)
    for d in range(1, nm):
        arrive(tables_row.at[x_peer(nm - d)], table_sems.at[0, d], x_id(d))
    for d in range(1, ny):
        send(tables_row, tables_all.at[y], table_sems.at[1, d], y_id(d))
    row_copy = pltpu.make_async_copy(tables_row, sources, local_sems.at[0])
    row_copy.start()
    tables_all[y] = tables_row[...]
    sums = mix_and_sum(0, regroup_end(0))
    size = jnp.sqrt(sums[0:1])
    shrink = 1.0 / size
    round_mixed(lambda k: raw[0, k] * shrink)
    loads[2].wait()
    loads[3].wait()

    def know_row():
        row_copy.wait()

    def know_all():
        for d in range(1, ny):
            arrive(tables_all.at[y_peer(ny - d)], table_sems.at[1, d], y_id(d))
        all_copy = pltpu.make_async_copy(tables_all, tables, local_sems.at[1])
        all_copy.start()
        all_copy.wait()

    far_and_near(0, know_row, know_all)

    first, second = applied.at[0], applied.at[1]
    complete(0)
    sum_start(1, pack([dot_lanes(first, source_ref), dot_lanes(first, first)]))
    regroup_start(1, far_sum.at[0])
    sum_second(1)
    far = regroup_end(1)
    sums = mix_and_sum(1, far + near_out[0].reshape(modes_total, width))
    h00 = sums[0:1] * shrink
    h10 = jnp.sqrt(jnp.maximum(sums[1:2] - h00 * h00, 0.0))
    lean = h00 * shrink
    shrink_1 = 1.0 / h10
    round_mixed(lambda k: (raw[1, k] - lean * raw[0, k]) * shrink_1)
    far_and_near(1)
    complete(1)

    def basis_0(t):
        return cell_block(source_ref, t) * shrink

    def basis_1(t):
        return (cell_block(first, t) - lean * cell_block(source_ref, t)) * shrink_1

    sum_start(
        2,
        pack(
            [
                lanes_of(lambda t: cell_block(second, t) * basis_0(t)),
                lanes_of(lambda t: cell_block(second, t) * basis_1(t)),
                lanes_of(lambda t: cell_block(second, t) * cell_block(second, t)),
                lanes_of(lambda t: basis_0(t) * basis_1(t)),
                lanes_of(lambda t: basis_1(t) * basis_1(t)),
            ]
        ),
    )
    sum_second(2)
    sum_third(2)
    sums = sum_end(2)
    h01, cross = sums[0:1], sums[3:4]
    h11 = sums[1:2] - h01 * cross
    h21 = jnp.sqrt(
        jnp.maximum(
            sums[2:3]
            - 2.0 * h01 * h01
            - 2.0 * h11 * sums[1:2]
            + h01 * h01
            + h11 * h11 * sums[4:5]
            + 2.0 * h01 * h11 * cross,
            0.0,
        )
    )

    r00 = jnp.sqrt(h00 * h00 + h10 * h10)
    cos0, sin0 = h00 / r00, h10 / r00
    g1 = -sin0 * size
    g0 = cos0 * size
    r01 = cos0 * h01 + sin0 * h11
    low = cos0 * h11 - sin0 * h01
    r11 = jnp.sqrt(low * low + h21 * h21)
    g1 = (low / r11) * g1
    y1 = g1 / r11
    y0 = (g0 - r01 * y1) / r00
    grow = size / h21
    for t in range(slab):
        v0, v1 = basis_0(t), basis_1(t)
        solution_ref[:, t * block : (t + 1) * block] = y0 * v0 + y1 * v1
        next_ref[:, t * block : (t + 1) * block] = (cell_block(second, t) - h01 * v0 - h11 * v1) * grow

    for copy in started:
        copy.wait_send()


def body(cells_y, cells_z, adjoint_source, coupling, diag_blocks, off_blocks, owner_cells, target_block):
    nm = lax.axis_size("modes")
    blocks_here, terms, block = diag_blocks.shape[:3]
    modes_total = coupling.shape[1]
    entries = terms * blocks_here
    rows = modes_total // nm
    slab = nm * blocks_here
    width = blocks_here * block
    dims = (cells_y, cells_z, nm, terms, blocks_here)
    f32, bf16 = jnp.float32, jnp.bfloat16
    chunk_count = -(-entries // cells_y)
    dma = pltpu.SemaphoreType.DMA
    vmem = pl.BlockSpec(memory_space=pltpu.VMEM)
    smem = pl.BlockSpec(memory_space=pltpu.SMEM)
    anywhere = pl.BlockSpec(memory_space=pl.ANY)
    return pl.pallas_call(
        functools.partial(kernel, dims),
        out_shape=[jax.ShapeDtypeStruct(adjoint_source.shape, f32)] * 2,
        in_specs=[smem, smem] + [anywhere] * 4,
        out_specs=[vmem, vmem],
        scratch_shapes=[
            pltpu.VMEM((rows, slab * block), f32),
            pltpu.VMEM((terms, modes_total, modes_total), f32),
            pltpu.VMEM((entries, block, block), bf16),
            pltpu.VMEM((entries, block, block), bf16),
            dma((4,)),
            pltpu.SMEM((entries,), jnp.int32),
            pltpu.VMEM((1, 128), jnp.int32),
            pltpu.VMEM((nm, 1, 128), jnp.int32),
            pltpu.VMEM((cells_y, nm, 1, 128), jnp.int32),
            pltpu.SMEM((nm, 1, 128), jnp.int32),
            pltpu.SMEM((cells_y, nm, 1, 128), jnp.int32),
            pltpu.VMEM((2, nm, rows, width), f32),
            pltpu.VMEM((2, terms, modes_total, width), f32),
            pltpu.VMEM((entries, modes_total, block), bf16),
            pltpu.VMEM((2, entries, nm, rows, block), f32),
            pltpu.VMEM((nm, entries, rows, block), f32),
            pltpu.VMEM((nm, entries, rows, block), f32),
            pltpu.VMEM((2, nm, entries + 1, rows, block), f32),
            pltpu.VMEM((2, cells_z, cells_y, nm, rows, block), f32),
            pltpu.VMEM((2, cells_z, cells_y, nm, rows, block), f32),
            pltpu.VMEM((2, cells_z, slab, rows, block), f32),
            pltpu.VMEM((2, 2, cells_z, slab, rows, block), f32),
            pltpu.VMEM((2, nm, rows, width), f32),
            pltpu.VMEM((2, nm, rows, width), f32),
            pltpu.VMEM((2, rows, slab * block), f32),
            pltpu.VMEM((2, rows, slab * block), f32),
            pltpu.VMEM((3, 3, 8, 128), f32),
            pltpu.VMEM((3, nm, 8, 128), f32),
            pltpu.VMEM((3, cells_y, 8, 128), f32),
            pltpu.VMEM((3, cells_z, 8, 128), f32),
            dma((2, max(nm, cells_y), 2)),
            dma((2,)),
            dma((2, nm, 2)),
            dma((2, chunk_count, nm, 2)),
            dma((2, cells_z, cells_y, 2)),
            dma((2, 2, cells_z, 2)),
            dma((2, nm, 2)),
            dma((3, nm, 2)),
            dma((3, cells_y, 2)),
            dma((3, cells_z, 2)),
        ],
        compiler_params=pltpu.CompilerParams(
            collective_id=0, has_side_effects=True, vmem_limit_bytes=62 * 1024 * 1024
        ),
    )(
        owner_cells.transpose(0, 2, 1),
        target_block,
        adjoint_source,
        coupling,
        diag_blocks.reshape(entries, block, block),
        off_blocks.reshape(entries, block, block),
    )


def solution(mesh, cells_z=8):
    cells_y = mesh.shape["cells"] // cells_z
    placed = (
        P("modes", "cells"),
        P(),
        P(("cells", "modes"), None, None, None),
        P(("cells", "modes"), None, None, None),
        P(("cells", "modes"), None, None),
        P(("cells", "modes"), None),
    )
    return jax.shard_map(
        functools.partial(body, cells_y, cells_z),
        mesh=mesh,
        in_specs=placed,
        out_specs=(P("modes", "cells"), P("modes", "cells")),
        check_vma=False,
    )
```
